256 devices in a mesh: group: 4 (over y_hi, core), tp: 64 (over x, z, y_lo).
Axes of the slice: x: 4, y: 4 (y_hi: 2, y_lo: 2; y = y_hi * 2 + y_lo), z: 8, core: 2. Of those that a mesh axis runs over, the one named last changes fastest.
Arguments:
- tokens: bfloat16 [512, 8192], P(('group', 'tp')), may hold values from -7 to 7
- sequence_numbers: int32 [4, 128], P('group'), may hold values from 0 to 3, never falling along the last dimension, each value on 1 to 64 neighbouring positions
- query_projection_weight: bfloat16 [8192, 8192], P(None, 'tp'), may hold values from -1.1 to 1.1
- key_projection_weight: bfloat16 [8192, 1024], P(None, 'tp'), may hold values from -0.36 to 0.36
- value_projection_weight: bfloat16 [8192, 1024], P(None, 'tp'), may hold values from -0.0625 to 0.0625
- output_projection_weight: bfloat16 [8192, 8192], P('tp'), may hold values from -0.0625 to 0.0625
- attention_norm_gain: float32 [8192], replicated, may hold values from 0.1 to 1.9
- closing_norm_gain: float32 [8192], replicated, may hold values from 0.1 to 1.9
- projector: bfloat16 [8192, 3584], P('tp'), may hold values from -0.0625 to 0.0625
- student_hidden_rows: bfloat16 [512, 3584], P(('group', 'tp')), may hold values from -6 to 6
- student_norm_gain: float32 [3584], replicated, may hold values from 0.1 to 1.9
- adapter_down_map: bfloat16 [3584, 64], replicated, may hold values from -0.09375 to 0.09375
- adapter_up_map: bfloat16 [64, 3584], replicated, may hold values from -0.75 to 0.75
Outputs:
- token_loss: float32 [512], P(('group', 'tp'))
- grad_down: float32 [3584, 64], replicated
- grad_up: float32 [64, 3584], replicated
The draws below stay inside these ranges and needn't reach their ends.
All inputs are finite; a program needn't handle non-finite values.
Results may differ from the reference program's by a relative error of at most 0.0045.
Values may be sent and summed in bfloat16 or wider, within the bound.
No kernel may reach another device: no remote copies, remote signals or barrier semaphores. Data moves between devices by JAX's collectives and lax.ppermute only.
A program may use at most 64 MiB of HBM per device.

```python
import math
import jax
import jax.numpy as jnp
import numpy as np
from jax import lax

D = 8192
H = 64
KV = 8
HD = 128
STUDENT_WIDTH = 3584
ADAPTER_RANK = 64
SEGS = 4
TOK_G = 128
TOKENS = 512
N_GROUP = 4


def key_columns(key):
    values = jax.random.truncated_normal(key, -4.0, 4.0, (D, HD * KV), jnp.float32)
    return values * (1.0 / math.sqrt(D))


def draw_key_projection_weight(key, part):
    shared = key_columns(key)
    return shared.astype(jnp.bfloat16)


def draw_query_projection_weight(key, part):
    key = jax.random.fold_in(key, 32)
    own_key = jax.random.fold_in(key, 0)
    values = jax.random.truncated_normal(own_key, -4.0, 4.0, (D, H * HD), jnp.float32) * (1.0 / math.sqrt(D))
    return values.astype(jnp.bfloat16)


def draw_tokens(key, part):
    key = jax.random.fold_in(key, 33)
    base_key = jax.random.fold_in(key, 0)
    values = jax.random.truncated_normal(base_key, -6.0, 6.0, (TOKENS, D), jnp.float32)
    return values.astype(jnp.bfloat16)


def steps_of(stream_key, extent, cuts, least, top_value):
    factor_of = 1.0
    for position, blocks in cuts:
        steps = jax.random.uniform(jax.random.fold_in(jax.random.fold_in(stream_key, 6), position), (blocks,), jnp.float32, least / len(cuts), top_value / len(cuts))
        factor_of = factor_of * jnp.repeat(jnp.exp(steps), extent[position] // blocks).reshape((-1,) + (1,) * (len(extent) - 1 - position))
    return factor_of


def profile(amount, total, most, slope):
    weights = [(1 << 20) // math.isqrt(standing ** slope) + 1 for standing in range(2, amount + 1)]
    rest, counts = total - most - (amount - 1), [1] * (amount - 1)
    while rest > 0:
        movable = [i for i in range(amount - 1) if counts[i] < most]
        pool, left = sum([weights[i] for i in movable]), rest
        for i in movable:
            addition = min(most - counts[i], max(1, left * weights[i] // pool), rest)
            counts[i] = counts[i] + addition
            rest = rest - addition
    return np.array([most] + counts)


def uneven_parts(key, amount, total, limit, lean):
    if amount == 2:
        one = jax.random.randint(key, (), max(1, total - limit), min(limit, total - 1) + 1)
        return jnp.stack([one, total - one])
    lengths = jnp.asarray(profile(amount, total, limit, lean), jnp.int32)
    couples = (amount - 1) // 2
    giver, sink = lengths[1:1 + 2 * couples:2], lengths[2:2 + 2 * couples:2]
    margin = jnp.minimum(giver - 1, limit - sink)
    shifted = jax.random.randint(jax.random.fold_in(key, 1), (couples,), 0, 1 << 20) % (margin + 1)
    lengths = lengths.at[1:1 + 2 * couples:2].set(giver - shifted).at[2:2 + 2 * couples:2].set(sink + shifted)
    return lengths[jax.random.permutation(jax.random.fold_in(key, 2), amount)]


def scatter_about(key, shape, deviation, reach, pieces=(), kind=jnp.bfloat16):
    result = deviation * jax.random.normal(key, shape, jnp.float32)
    if pieces:
        result = result * steps_of(key, shape, pieces, -0.22, 0.18)
    return jnp.clip(result, -reach, reach).astype(kind)


def setup_inputs(seed: int = 0) -> dict:
    seeds = jax.random.split(jax.random.key(seed), 14)
    tokens = draw_tokens(jax.random.fold_in(seeds[13], 71), 0)
    sequence_numbers = jax.vmap(lambda own: jnp.searchsorted(jnp.cumsum(uneven_parts(own, SEGS, TOK_G, TOK_G // 2, 2)), jnp.arange(TOK_G), side="right"))(jax.random.split(seeds[1], N_GROUP)).reshape((N_GROUP, TOK_G)).astype(jnp.int32)
    query_projection_weight = draw_query_projection_weight(jax.random.fold_in(seeds[13], 71), 0)
    key_projection_weight = draw_key_projection_weight(jax.random.fold_in(seeds[13], 71), 0)
    value_projection_weight = scatter_about(seeds[4], (D, HD * KV), D ** -0.5, 0.0625, ((1, 64),))
    output_projection_weight = scatter_about(seeds[5], (H * HD, D), (H * HD) ** -0.5, 0.0625, ((0, 64),))
    attention_norm_gain = jnp.clip(1.0 + 0.18 * jax.random.normal(seeds[6], (D,), jnp.float32), 0.1, 1.9)
    closing_norm_gain = jnp.clip(1.0 + 0.18 * jax.random.normal(seeds[7], (D,), jnp.float32), 0.1, 1.9)
    projector = scatter_about(seeds[8], (D, STUDENT_WIDTH), D ** -0.5, 0.0625, ((0, 64),))
    student_hidden_rows = scatter_about(seeds[9], (TOKENS, STUDENT_WIDTH), 1.0, 6.0, ((0, 256),))
    student_norm_gain = jnp.clip(1.0 + 0.18 * jax.random.normal(seeds[10], (STUDENT_WIDTH,), jnp.float32), 0.1, 1.9)
    adapter_down_map = scatter_about(seeds[11], (STUDENT_WIDTH, ADAPTER_RANK), STUDENT_WIDTH ** -0.5, 0.09375)
    adapter_up_map = scatter_about(seeds[12], (ADAPTER_RANK, STUDENT_WIDTH), ADAPTER_RANK ** -0.5, 0.75)
    return {"tokens": tokens, "sequence_numbers": sequence_numbers, "query_projection_weight": query_projection_weight, "key_projection_weight": key_projection_weight, "value_projection_weight": value_projection_weight, "output_projection_weight": output_projection_weight, "attention_norm_gain": attention_norm_gain, "closing_norm_gain": closing_norm_gain, "projector": projector, "student_hidden_rows": student_hidden_rows, "student_norm_gain": student_norm_gain, "adapter_down_map": adapter_down_map, "adapter_up_map": adapter_up_map}


eps = 1e-06

def rms_norm(values, gain):
    mean_sq = lax.optimization_barrier(jnp.mean(values * values, axis=-1, keepdims=True))
    return values * lax.rsqrt(mean_sq + eps) * gain

def reference(tokens, sequence_numbers, query_projection_weight, key_projection_weight, value_projection_weight, output_projection_weight, attention_norm_gain, closing_norm_gain, projector, student_hidden_rows, student_norm_gain, adapter_down_map, adapter_up_map):
    highest_precision = lax.Precision.HIGHEST
    grad_down = jnp.zeros((STUDENT_WIDTH, ADAPTER_RANK), jnp.float32)
    grad_up = jnp.zeros((ADAPTER_RANK, STUDENT_WIDTH), jnp.float32)
    losses = []
    positions = jnp.arange(TOK_G, dtype=jnp.int32)
    for batch in range(N_GROUP):
        rows = tokens[batch * TOK_G:(batch + 1) * TOK_G]
        seg = sequence_numbers[batch]
        normed = rms_norm(rows.astype(jnp.float32), attention_norm_gain).astype(jnp.bfloat16)
        query = jnp.dot(normed, query_projection_weight, preferred_element_type=jnp.float32).astype(jnp.bfloat16).reshape(TOK_G, H, HD)
        key = jnp.dot(normed, key_projection_weight, preferred_element_type=jnp.float32).astype(jnp.bfloat16).reshape(TOK_G, HD, KV).transpose(0, 2, 1)
        value = jnp.dot(normed, value_projection_weight, preferred_element_type=jnp.float32).astype(jnp.bfloat16).reshape(TOK_G, HD, KV).transpose(0, 2, 1)
        key_all = jnp.repeat(key, H // KV, axis=1).astype(jnp.float32)
        value_all = jnp.repeat(value, H // KV, axis=1).astype(jnp.float32)
        scores = jnp.einsum('qhd,khd->hqk', query.astype(jnp.float32), key_all) / jnp.sqrt(jnp.float32(HD))
        allowed = (positions[:, None] >= positions[None, :]) & (seg[:, None] == seg[None, :])
        scores = jnp.where(allowed[None], scores, jnp.float32(-1e+30))
        weights = jax.nn.softmax(scores, axis=-1).astype(jnp.bfloat16)
        context = jnp.einsum('hqk,khd->qhd', weights.astype(jnp.float32), value_all).astype(jnp.bfloat16).reshape(TOK_G, H * HD)
        resid = rows.astype(jnp.float32) + jnp.dot(context, output_projection_weight, preferred_element_type=jnp.float32)
        hidden = rms_norm(resid, closing_norm_gain).astype(jnp.bfloat16)
        target_output = jnp.dot(hidden, projector, preferred_element_type=jnp.float32)
        student_output = student_hidden_rows[batch * TOK_G:(batch + 1) * TOK_G]
        student_normed_rows = rms_norm(student_output.astype(jnp.float32), student_norm_gain).astype(jnp.bfloat16)
        lowrank_update = jnp.dot(student_normed_rows, adapter_down_map, preferred_element_type=jnp.float32).astype(jnp.bfloat16)
        difference_rows = student_output.astype(jnp.float32) + jnp.dot(lowrank_update, adapter_up_map, preferred_element_type=jnp.float32) - target_output
        losses.append(lax.optimization_barrier(jnp.mean(difference_rows * difference_rows, axis=1)))
        scaled_rows = difference_rows / jnp.sqrt(jnp.float32(TOKENS))
        grad_up = grad_up + jnp.dot(lowrank_update.astype(jnp.float32).T, scaled_rows, precision=highest_precision, preferred_element_type=jnp.float32)
        backward_pass = jnp.dot(scaled_rows, adapter_up_map.astype(jnp.float32).T, precision=highest_precision, preferred_element_type=jnp.float32)
        grad_down = grad_down + jnp.dot(student_normed_rows.astype(jnp.float32).T, backward_pass, precision=highest_precision, preferred_element_type=jnp.float32)
    return (jnp.concatenate(losses, axis=0), grad_down, grad_up)
```

```python
import jax
import jax.numpy as jnp
import numpy as np
from jax import lax
from jax.sharding import Mesh
from jax.sharding import PartitionSpec as P

D = 8192
H = 64
KV = 8
HD = 128
WIDTH = 3584
RANK = 64
TP = ("x", "z", "yl")
ALL = ("yh", "core", "x", "z", "yl")
NEAR = ("x", "yl")
FAR = ("yh", "core", "z")
SPREAD = NEAR + FAR

eps = 1e-06
f32 = jnp.float32
bf16 = jnp.bfloat16
highest = lax.Precision.HIGHEST


def rms_norm(values, gain):
    mean_sq = jnp.mean(values * values, axis=-1, keepdims=True)
    return values * lax.rsqrt(mean_sq + eps) * gain


def exchange(blocks, axes):
    return lax.all_to_all(blocks, axes, split_axis=0, concat_axis=0, tiled=True)


def from_x(block, step):
    return lax.ppermute(block, "x", [((i + step) % 4, i) for i in range(4)])


def from_yl(block):
    return lax.ppermute(block, "yl", [(0, 1), (1, 0)])


def shards(
    tokens,
    sequence_numbers,
    query_projection_weight,
    key_projection_weight,
    value_projection_weight,
    output_projection_weight,
    attention_norm_gain,
    closing_norm_gain,
    projector,
    student_hidden_rows,
    student_norm_gain,
    adapter_down_map,
    adapter_up_map,
):
    tp_index = lax.axis_index(TP)
    colour = lax.rem(lax.axis_index("x") + 2 * lax.axis_index("yl"), 4)

    with jax.named_scope("tokens"):
        normed = rms_norm(tokens.astype(f32), attention_norm_gain).astype(bf16)
        quarters = normed.reshape(2, 4, D // 4).transpose(1, 0, 2)
        by_colour = jnp.stack([quarters, jnp.roll(quarters, -2, axis=0)], axis=1)
        by_colour = jnp.broadcast_to(by_colour[:, None], (4, 8, 2, 2, D // 4)).reshape(64, 2, D // 4)
        raw = tokens.reshape(2, 64, HD).transpose(1, 0, 2)
        got = exchange(jnp.concatenate([by_colour, raw], axis=2), TP)
        mine = got[:, :, : D // 4].reshape(128, D // 4)
        raw_cols = got[:, :, D // 4 :].reshape(128, HD)
        parts = [mine, from_x(mine, 1), from_yl(mine), from_x(mine, 3)]

    with jax.named_scope("project"):
        query = jnp.zeros((128, HD), f32)
        key_t = jnp.zeros((16, 128), f32)
        value_t = jnp.zeros((16, 128), f32)
        contract = (((0,), (1,)), ((), ()))
        for step, part in enumerate(parts):
            start = lax.rem(colour + step, 4) * (D // 4)

            def rows(w, start=start):
                return lax.dynamic_slice_in_dim(w, start, D // 4, 0)

            query += jnp.dot(part, rows(query_projection_weight), preferred_element_type=f32)
            key_t += lax.dot_general(rows(key_projection_weight), part, contract, preferred_element_type=f32)
            value_t += lax.dot_general(rows(value_projection_weight), part, contract, preferred_element_type=f32)
        query = query.astype(bf16)

    with jax.named_scope("keys"):
        both = jnp.stack([key_t, value_t]).astype(bf16).reshape(2, 2, KV, 128)
        by_head = both.transpose(2, 0, 1, 3).reshape(KV, 1, 4, 128)
        both = exchange(jnp.broadcast_to(by_head, (KV, 8, 4, 128)).reshape(64, 4, 128), TP)
        both = both.reshape(64, 2, 2, 128)
        key_t = both[:, 0].reshape(HD, 128)
        value_t = both[:, 1].reshape(HD, 128)

    with jax.named_scope("attention"):
        scores = jnp.dot(query, key_t, preferred_element_type=f32) / jnp.sqrt(f32(HD))
        positions = lax.iota(jnp.int32, 128)
        seg = sequence_numbers[0]
        allowed = (positions[:, None] >= positions[None, :]) & (seg[:, None] == seg[None, :])
        scores = jnp.where(allowed, scores, f32(-1e30))
        weights = jax.nn.softmax(scores, axis=-1).astype(bf16)
        context = lax.dot_general(weights, value_t, (((1,), (1,)), ((), ())), preferred_element_type=f32).astype(bf16)

    with jax.named_scope("output"):
        twice = jnp.concatenate([context, context], axis=0)
        turned = lax.dynamic_slice_in_dim(twice, colour * 32, 128, 0)
        partial = jnp.dot(turned, output_projection_weight, preferred_element_type=f32).reshape(4, 32, D)
        sent = partial.astype(bf16)
        total = partial[0] + from_x(sent[1], 3).astype(f32) + from_yl(sent[2]).astype(f32) + from_x(sent[3], 1).astype(f32)
        columns = total.astype(bf16).reshape(32, 64, HD).transpose(1, 0, 2)
        columns = exchange(columns, TP).reshape(4, 8, 2, 32, HD)
        columns = jnp.sum(columns.astype(f32), axis=1)
        summed = (columns[:, 0] + jnp.roll(columns[:, 1], 2, axis=0)).reshape(128, HD)
        resid = raw_cols.astype(f32) + summed

    with jax.named_scope("target"):
        squares = jnp.sum(resid * resid, axis=1)
        high = squares.astype(bf16)
        low = (squares - high.astype(f32)).astype(bf16)
        gain_cols = lax.dynamic_slice_in_dim(closing_norm_gain, tp_index * HD, HD, 0)
        features = (resid * gain_cols).astype(bf16)
        projected = jnp.dot(features, projector, preferred_element_type=f32).astype(bf16)
        tail = jnp.pad(jnp.stack([high, low], axis=1), ((0, 0), (0, 126)))
        rows_out = jnp.concatenate([projected, tail], axis=1).reshape(64, 2, WIDTH + 128)
        rows_in = jnp.sum(exchange(rows_out, TP).astype(f32), axis=0)
        squares = rows_in[:, WIDTH] + rows_in[:, WIDTH + 1]
        target = rows_in[:, :WIDTH] * lax.rsqrt(squares / D + eps)[:, None]

    with jax.named_scope("student"):
        student = student_hidden_rows.astype(f32)
        student_normed = rms_norm(student, student_norm_gain).astype(bf16)
        lowrank = jnp.dot(student_normed, adapter_down_map, preferred_element_type=f32).astype(bf16)
        reached = student + jnp.dot(lowrank, adapter_up_map, preferred_element_type=f32)
        diff = reached - target
        token_loss = jnp.mean(diff * diff, axis=1)
        scaled = diff / jnp.sqrt(f32(512))
        back = lax.dot_general(
            scaled, adapter_up_map.astype(f32), (((1,), (1,)), ((), ())), precision=highest, preferred_element_type=f32
        )

    with jax.named_scope("columns"):
        across = jnp.concatenate([scaled.astype(bf16).reshape(28, 256), student_normed.reshape(28, 256)], axis=0)
        across = jnp.pad(across, ((0, 72), (0, 0))).T.reshape(256, 1, 128)
        same = jnp.stack([back.astype(bf16).reshape(128), lowrank.reshape(128)])
        message = jnp.concatenate([across, jnp.broadcast_to(same[None], (256, 2, 128))], axis=1)
        message = exchange(message, SPREAD)
        gram = lax.dot_general(
            message[:, 0], message[:, 1:].reshape(256, 256), (((0,), (0,)), ((), ())), preferred_element_type=f32
        )
        up_part = gram[0:14, 128:192] + gram[14:28, 192:256]
        down_part = gram[28:42, 0:64] + gram[42:56, 64:128]

    with jax.named_scope("gradients"):
        chunk = jnp.concatenate([down_part, up_part], axis=1).astype(bf16)
        far = exchange(jnp.broadcast_to(chunk, (32, 14, 128)), FAR)
        whole = exchange(jnp.broadcast_to(far, (8, 32, 14, 128)), NEAR).reshape(256, 14, 128)
        whole = whole.astype(f32)
        grad_down = whole[:, :, :64].transpose(1, 0, 2).reshape(WIDTH, RANK)
        grad_up = whole[:, :, 64:].transpose(2, 1, 0).reshape(RANK, WIDTH)
    return (token_loss, grad_down, grad_up)


def solution(mesh):
    fine = Mesh(np.asarray(mesh.devices).reshape(2, 2, 4, 8, 2), ALL)
    return jax.shard_map(
        shards,
        mesh=fine,
        in_specs=(
            P(ALL, None),
            P(("yh", "core"), None),
            P(None, TP),
            P(None, TP),
            P(None, TP),
            P(TP, None),
            P(),
            P(),
            P(TP, None),
            P(ALL, None),
            P(),
            P(),
            P(),
        ),
        out_specs=(P(ALL), P(), P()),
        check_vma=False,
    )
```

```python
import jax
import jax.numpy as jnp
import numpy as np
from jax import lax
from jax.sharding import Mesh
from jax.sharding import PartitionSpec as P

D = 8192
H = 64
KV = 8
HD = 128
WIDTH = 3584
RANK = 64
TP = ("x", "z", "yl")
ALL = ("yh", "core", "x", "z", "yl")
WIDE = ("yh", "core", "x", "yl")

eps = 1e-06
f32 = jnp.float32
bf16 = jnp.bfloat16
highest = lax.Precision.HIGHEST


def rms_norm(values, gain):
    mean_sq = jnp.mean(values * values, axis=-1, keepdims=True)
    return values * lax.rsqrt(mean_sq + eps) * gain


def exchange(blocks, axes):
    return lax.all_to_all(blocks, axes, split_axis=0, concat_axis=0, tiled=True)


def from_x(block, step):
    return lax.ppermute(block, "x", [((i + step) % 4, i) for i in range(4)])


def from_yl(block):
    return lax.ppermute(block, "yl", [(0, 1), (1, 0)])


def shards(
    tokens,
    sequence_numbers,
    query_projection_weight,
    key_projection_weight,
    value_projection_weight,
    output_projection_weight,
    attention_norm_gain,
    closing_norm_gain,
    projector,
    student_hidden_rows,
    student_norm_gain,
    adapter_down_map,
    adapter_up_map,
):
    tp_index = lax.axis_index(TP)
    colour = lax.rem(lax.axis_index("x") + 2 * lax.axis_index("yl"), 4)

    with jax.named_scope("tokens"):
        quarters = tokens.reshape(2, 4, D // 4).transpose(1, 0, 2)
        by_colour = jnp.stack([quarters, jnp.roll(quarters, -2, axis=0)], axis=1)
        by_colour = jnp.broadcast_to(by_colour[:, None], (4, 8, 2, 2, D // 4)).reshape(64, 2, D // 4)
        mine = exchange(by_colour, TP).reshape(128, D // 4)
        parts = [mine, from_x(mine, 1), from_yl(mine), from_x(mine, 3)]
        at = lax.rem(tp_index, 16) * HD
        raw_cols = jnp.where(
            lax.axis_index("yl") == 0,
            lax.dynamic_slice_in_dim(parts[0], at, HD, 1),
            lax.dynamic_slice_in_dim(parts[2], at, HD, 1),
        )

    with jax.named_scope("project"):
        query = jnp.zeros((128, HD), f32)
        key_t = jnp.zeros((16, 128), f32)
        value_t = jnp.zeros((16, 128), f32)
        squares = jnp.zeros((128,), f32)
        contract = (((0,), (1,)), ((), ()))
        for step, part in enumerate(parts):
            start = lax.rem(colour + step, 4) * (D // 4)

            def rows(w, start=start):
                return lax.dynamic_slice_in_dim(w, start, D // 4, 0)

            wide = part.astype(f32)
            squares += jnp.sum(wide * wide, axis=1)
            part = (wide * rows(attention_norm_gain)).astype(bf16)
            query += jnp.dot(part, rows(query_projection_weight), preferred_element_type=f32)
            key_t += lax.dot_general(rows(key_projection_weight), part, contract, preferred_element_type=f32)
            value_t += lax.dot_general(rows(value_projection_weight), part, contract, preferred_element_type=f32)
        scale = lax.rsqrt(squares / D + eps)
        query = (query * scale[:, None]).astype(bf16)
        key_t = key_t * scale[None, :]
        value_t = value_t * scale[None, :]

    with jax.named_scope("keys"):
        both = jnp.stack([key_t, value_t]).astype(bf16).reshape(2, 2, KV, 128)
        by_head = both.transpose(2, 0, 1, 3).reshape(KV, 1, 4, 128)
        both = exchange(jnp.broadcast_to(by_head, (KV, 8, 4, 128)).reshape(64, 4, 128), TP)
        both = both.reshape(64, 2, 2, 128)
        key_t = both[:, 0].reshape(HD, 128)
        value_t = both[:, 1].reshape(HD, 128)

    with jax.named_scope("attention"):
        scores = jnp.dot(query, key_t, preferred_element_type=f32) / jnp.sqrt(f32(HD))
        positions = lax.iota(jnp.int32, 128)
        seg = sequence_numbers[0]
        allowed = (positions[:, None] >= positions[None, :]) & (seg[:, None] == seg[None, :])
        scores = jnp.where(allowed, scores, f32(-1e30))
        weights = jax.nn.softmax(scores, axis=-1).astype(bf16)
        context = lax.dot_general(weights, value_t, (((1,), (1,)), ((), ())), preferred_element_type=f32).astype(bf16)

    with jax.named_scope("output"):
        twice = jnp.concatenate([context, context], axis=0)
        turned = lax.dynamic_slice_in_dim(twice, colour * 32, 128, 0)
        partial = jnp.dot(turned, output_projection_weight, preferred_element_type=f32).reshape(4, 32, D)
        sent = partial.astype(bf16)
        total = partial[0] + from_x(sent[1], 3).astype(f32) + from_yl(sent[2]).astype(f32) + from_x(sent[3], 1).astype(f32)
        columns = total.astype(bf16).reshape(32, 64, HD).transpose(1, 0, 2)
        columns = exchange(columns, TP).reshape(4, 8, 2, 32, HD)
        columns = jnp.sum(columns.astype(f32), axis=1)
        summed = (columns[:, 0] + jnp.roll(columns[:, 1], 2, axis=0)).reshape(128, HD)
        resid = raw_cols.astype(f32) + summed

    with jax.named_scope("target"):
        squares = jnp.sum(resid * resid, axis=1)
        high = squares.astype(bf16)
        low = (squares - high.astype(f32)).astype(bf16)
        gain_cols = lax.dynamic_slice_in_dim(closing_norm_gain, tp_index * HD, HD, 0)
        features = (resid * gain_cols).astype(bf16)
        projected = jnp.dot(features, projector, preferred_element_type=f32).astype(bf16)
        tail = jnp.pad(jnp.stack([high, low], axis=1), ((0, 0), (0, 126)))
        rows_out = jnp.concatenate([projected, tail], axis=1).reshape(64, 2, WIDTH + 128)
        rows_in = jnp.sum(exchange(rows_out, TP).astype(f32), axis=0)
        squares = rows_in[:, WIDTH] + rows_in[:, WIDTH + 1]
        target = rows_in[:, :WIDTH] * lax.rsqrt(squares / D + eps)[:, None]

    with jax.named_scope("student"):
        student = student_hidden_rows.astype(f32)
        student_normed = rms_norm(student, student_norm_gain).astype(bf16)
        lowrank = jnp.dot(student_normed, adapter_down_map, preferred_element_type=f32).astype(bf16)
        reached = student + jnp.dot(lowrank, adapter_up_map, preferred_element_type=f32)
        diff = reached - target
        token_loss = jnp.mean(diff * diff, axis=1)
        scaled = diff / jnp.sqrt(f32(512))
        back = lax.dot_general(
            scaled, adapter_up_map.astype(f32), (((1,), (1,)), ((), ())), precision=highest, preferred_element_type=f32
        )

    with jax.named_scope("columns"):

        def groups(v):
            return v.reshape(2, 28, 128).transpose(1, 0, 2)

        left = jnp.concatenate([groups(student_normed), groups(scaled.astype(bf16))], axis=1)
        left = jnp.pad(left, ((0, 4), (0, 0), (0, 0)))
        right = jnp.concatenate(
            [jnp.pad(back.astype(bf16), ((0, 0), (0, 64))), jnp.pad(lowrank, ((0, 0), (64, 0)))], axis=0
        )
        message = jnp.concatenate([left, jnp.broadcast_to(right, (32, 4, 128))], axis=1)
        message = jnp.broadcast_to(message[:, None], (32, 8, 8, 128)).reshape(256, 8, 128)
        message = exchange(message, WIDE + ("z",))
        chunk = lax.dot_general(
            message[:, 4:].reshape(1024, 128),
            message[:, :4].reshape(1024, 128),
            (((0,), (0,)), ((), ())),
            preferred_element_type=f32,
        ).astype(bf16)

    with jax.named_scope("gradients"):
        whole = exchange(jnp.broadcast_to(chunk, (32, 128, 128)), WIDE)[:28].astype(f32)
        grad_down = whole[:, :64].transpose(0, 2, 1).reshape(WIDTH, RANK)
        grad_up = whole[:, 64:].transpose(1, 0, 2).reshape(RANK, WIDTH)
    return (token_loss, grad_down, grad_up)


def solution(mesh):
    fine = Mesh(np.asarray(mesh.devices).reshape(2, 2, 4, 8, 2), ALL)
    return jax.shard_map(
        shards,
        mesh=fine,
        in_specs=(
            P(ALL, None),
            P(("yh", "core"), None),
            P(None, TP),
            P(None, TP),
            P(None, TP),
            P(TP, None),
            P(),
            P(),
            P(TP, None),
            P(ALL, None),
            P(),
            P(),
            P(),
        ),
        out_specs=(P(ALL), P(), P()),
        check_vma=False,
    )
```

```python
import jax
import jax.numpy as jnp
import numpy as np
from jax import lax
from jax.sharding import Mesh
from jax.sharding import PartitionSpec as P

D = 8192
H = 64
KV = 8
HD = 128
WIDTH = 3584
RANK = 64
TP = ("x", "z", "yl")
ALL = ("yh", "core", "x", "z", "yl")
WIDE = ("yh", "core", "x", "yl")

eps = 1e-06
f32 = jnp.float32
bf16 = jnp.bfloat16
highest = lax.Precision.HIGHEST


def rms_norm(values, gain):
    mean_sq = jnp.mean(values * values, axis=-1, keepdims=True)
    return values * lax.rsqrt(mean_sq + eps) * gain


def exchange(blocks, axes):
    return lax.all_to_all(blocks, axes, split_axis=0, concat_axis=0, tiled=True)


def from_x(block, step):
    return lax.ppermute(block, "x", [((i + step) % 4, i) for i in range(4)])


def from_yl(block):
    return lax.ppermute(block, "yl", [(0, 1), (1, 0)])


def pick_rows():
    pick = np.zeros((2, 4, 8, 2, 2, 4, 8, 2, 4, 2, 2), np.float32)
    for x in range(4):
        for yl in range(2):
            for step, (sx, syl) in enumerate([(x, yl), ((x + 1) % 4, yl), (x, 1 - yl), ((x + 3) % 4, yl)]):
                for z in range(8):
                    for part in range(2):
                        for e in range(2):
                            pick[part, x, z, yl, e, sx, z, syl, step, part, e] = 1
    return pick.reshape(256, 1024)


def shards(
    tokens,
    sequence_numbers,
    query_projection_weight,
    key_projection_weight,
    value_projection_weight,
    output_projection_weight,
    attention_norm_gain,
    closing_norm_gain,
    projector,
    student_hidden_rows,
    student_norm_gain,
    adapter_down_map,
    adapter_up_map,
):
    tp_index = lax.axis_index(TP)
    colour = lax.rem(lax.axis_index("x") + 2 * lax.axis_index("yl"), 4)

    with jax.named_scope("kv_weights"):
        columns = jnp.stack([key_projection_weight.T, value_projection_weight.T]).reshape(2, 2, KV, D)

        def features(w, step, axis):
            return lax.dynamic_slice_in_dim(w, lax.rem(colour + step, 4) * (D // 4), D // 4, axis)

        kv = [features(columns, step, 3).reshape(32, D // 4) for step in range(4)]
        kv = [kv[0], from_x(kv[1], 3), from_yl(kv[2]), from_x(kv[3], 1)]
        kv = jnp.stack(kv).reshape(16, KV, D // 4).transpose(1, 0, 2).reshape(128, D // 4)

    with jax.named_scope("tokens"):
        quarters = tokens.reshape(2, 4, D // 4).transpose(1, 0, 2)
        by_colour = jnp.stack([quarters, jnp.roll(quarters, -2, axis=0)], axis=1)
        by_colour = jnp.broadcast_to(by_colour[:, None], (4, 8, 2, 2, D // 4)).reshape(64, 2, D // 4)
        mine = exchange(by_colour, TP).reshape(128, D // 4)
        parts = [mine, from_x(mine, 1), from_yl(mine), from_x(mine, 3)]
        at = lax.rem(tp_index, 16) * HD
        raw_cols = jnp.where(
            lax.axis_index("yl") == 0,
            lax.dynamic_slice_in_dim(parts[0], at, HD, 1),
            lax.dynamic_slice_in_dim(parts[2], at, HD, 1),
        )

    with jax.named_scope("keys"):
        gained = (mine.astype(f32) * features(attention_norm_gain, 0, 0)).astype(bf16)
        served = lax.dot_general(kv, gained, (((1,), (1,)), ((), ())), preferred_element_type=f32).astype(bf16)
        served = jnp.broadcast_to(served.reshape(KV, 1, 16, 128), (KV, 8, 16, 128)).reshape(64, 16, 128)
        served = exchange(served, TP).reshape(1024, 128)
        both = jnp.dot(jnp.asarray(pick_rows(), bf16), served, preferred_element_type=f32)

    with jax.named_scope("project"):
        query = jnp.zeros((128, HD), f32)
        squares = jnp.zeros((128,), f32)
        for step, part in enumerate(parts):
            wide = part.astype(f32)
            squares += jnp.sum(wide * wide, axis=1)
            part = (wide * features(attention_norm_gain, step, 0)).astype(bf16)
            query += jnp.dot(part, features(query_projection_weight, step, 0), preferred_element_type=f32)
        scale = lax.rsqrt(squares / D + eps)
        query = (query * scale[:, None]).astype(bf16)
        key_t = (both[:128] * scale[None, :]).astype(bf16)
        value_t = (both[128:] * scale[None, :]).astype(bf16)

    with jax.named_scope("attention"):
        scores = jnp.dot(query, key_t, preferred_element_type=f32) / jnp.sqrt(f32(HD))
        positions = lax.iota(jnp.int32, 128)
        seg = sequence_numbers[0]
        allowed = (positions[:, None] >= positions[None, :]) & (seg[:, None] == seg[None, :])
        scores = jnp.where(allowed, scores, f32(-1e30))
        weights = jax.nn.softmax(scores, axis=-1).astype(bf16)
        context = lax.dot_general(weights, value_t, (((1,), (1,)), ((), ())), preferred_element_type=f32).astype(bf16)

    with jax.named_scope("output"):
        twice = jnp.concatenate([context, context], axis=0)
        turned = lax.dynamic_slice_in_dim(twice, colour * 32, 128, 0)
        partial = jnp.dot(turned, output_projection_weight, preferred_element_type=f32).reshape(4, 32, D)
        sent = partial.astype(bf16)
        total = partial[0] + from_x(sent[1], 3).astype(f32) + from_yl(sent[2]).astype(f32) + from_x(sent[3], 1).astype(f32)
        columns = total.astype(bf16).reshape(32, 64, HD).transpose(1, 0, 2)
        columns = exchange(columns, TP).reshape(4, 8, 2, 32, HD)
        columns = jnp.sum(columns.astype(f32), axis=1)
        summed = (columns[:, 0] + jnp.roll(columns[:, 1], 2, axis=0)).reshape(128, HD)
        resid = raw_cols.astype(f32) + summed

    with jax.named_scope("target"):
        squares = jnp.sum(resid * resid, axis=1)
        high = squares.astype(bf16)
        low = (squares - high.astype(f32)).astype(bf16)
        gain_cols = lax.dynamic_slice_in_dim(closing_norm_gain, tp_index * HD, HD, 0)
        features = (resid * gain_cols).astype(bf16)
        projected = jnp.dot(features, projector, preferred_element_type=f32).astype(bf16)
        tail = jnp.pad(jnp.stack([high, low], axis=1), ((0, 0), (0, 126)))
        rows_out = jnp.concatenate([projected, tail], axis=1).reshape(64, 2, WIDTH + 128)
        rows_in = jnp.sum(exchange(rows_out, TP).astype(f32), axis=0)
        squares = rows_in[:, WIDTH] + rows_in[:, WIDTH + 1]
        target = rows_in[:, :WIDTH] * lax.rsqrt(squares / D + eps)[:, None]

    with jax.named_scope("student"):
        student = student_hidden_rows.astype(f32)
        student_normed = rms_norm(student, student_norm_gain).astype(bf16)
        lowrank = jnp.dot(student_normed, adapter_down_map, preferred_element_type=f32).astype(bf16)
        reached = student + jnp.dot(lowrank, adapter_up_map, preferred_element_type=f32)
        diff = reached - target
        token_loss = jnp.mean(diff * diff, axis=1)
        scaled = diff / jnp.sqrt(f32(512))
        back = lax.dot_general(
            scaled, adapter_up_map.astype(f32), (((1,), (1,)), ((), ())), precision=highest, preferred_element_type=f32
        )

    with jax.named_scope("columns"):

        def groups(v):
            return v.reshape(2, 28, 128).transpose(1, 0, 2)

        left = jnp.concatenate([groups(student_normed), groups(scaled.astype(bf16))], axis=1)
        left = jnp.pad(left, ((0, 4), (0, 0), (0, 0)))
        right = jnp.concatenate([back.astype(bf16), lowrank], axis=1)
        message = jnp.concatenate([left, jnp.broadcast_to(right, (32, 2, 128))], axis=1)
        message = jnp.broadcast_to(message[:, None], (32, 8, 6, 128)).reshape(256, 6, 128)
        message = exchange(message, WIDE + ("z",))

        def product(i, j):
            return lax.dot_general(
                message[:, i], message[:, j], (((0,), (0,)), ((), ())), preferred_element_type=f32
            )

        down = product(4, 0) + product(5, 1)
        up = product(4, 2) + product(5, 3)
        chunk = jnp.concatenate([down[:64], up[64:]], axis=0).astype(bf16)

    with jax.named_scope("gradients"):
        whole = exchange(jnp.broadcast_to(chunk, (32, 128, 128)), WIDE)[:28].astype(f32)
        grad_down = whole[:, :64].transpose(0, 2, 1).reshape(WIDTH, RANK)
        grad_up = whole[:, 64:].transpose(1, 0, 2).reshape(RANK, WIDTH)
    return (token_loss, grad_down, grad_up)


def solution(mesh):
    fine = Mesh(np.asarray(mesh.devices).reshape(2, 2, 4, 8, 2), ALL)
    return jax.shard_map(
        shards,
        mesh=fine,
        in_specs=(
            P(ALL, None),
            P(("yh", "core"), None),
            P(None, TP),
            P(None, TP),
            P(None, TP),
            P(TP, None),
            P(),
            P(),
            P(TP, None),
            P(ALL, None),
            P(),
            P(),
            P(),
        ),
        out_specs=(P(ALL), P(), P()),
        check_vma=False,
    )
```

```python
import jax
import jax.numpy as jnp
import numpy as np
from jax import lax
from jax.experimental import pallas as pl
from jax.experimental.pallas import tpu as pltpu
from jax.sharding import Mesh
from jax.sharding import PartitionSpec as P

D = 8192
H = 64
KV = 8
HD = 128
WIDTH = 3584
RANK = 64
TP = ("x", "z", "yl")
ALL = ("yh", "core", "x", "z", "yl")
WIDE = ("yh", "core", "x", "yl")

eps = 1e-06
VMEM_MB = 24
f32 = jnp.float32
bf16 = jnp.bfloat16
highest = lax.Precision.HIGHEST


def rms_norm(values, gain):
    mean_sq = jnp.mean(values * values, axis=-1, keepdims=True)
    return values * lax.rsqrt(mean_sq + eps) * gain


def exchange(blocks, axes):
    return lax.all_to_all(blocks, axes, split_axis=0, concat_axis=0, tiled=True)


def from_x(block, step):
    return lax.ppermute(block, "x", [((i + step) % 4, i) for i in range(4)])


def from_yl(block):
    return lax.ppermute(block, "yl", [(0, 1), (1, 0)])


def pick_rows():
    pick = np.zeros((2, 4, 8, 2, 2, 4, 8, 2, 4, 2, 2), np.float32)
    for x in range(4):
        for yl in range(2):
            for step, (sx, syl) in enumerate([(x, yl), ((x + 1) % 4, yl), (x, 1 - yl), ((x + 3) % 4, yl)]):
                for z in range(8):
                    for part in range(2):
                        for e in range(2):
                            pick[part, x, z, yl, e, sx, z, syl, step, part, e] = 1
    return pick.reshape(256, 1024)


def gained(part_ref, gain_ref, start):
    wide = part_ref[...].astype(f32)
    squares = jnp.sum(wide * wide, axis=1, keepdims=True)
    return (wide * gain_ref[:, pl.ds(start, D // 4)]).astype(bf16), squares


def own_quarter(colour_ref, mine_ref, gain_ref, kv_ref, served_ref):
    part, _ = gained(mine_ref, gain_ref, pl.multiple_of(colour_ref[0] * (D // 4), D // 4))
    served = lax.dot_general(kv_ref[...], part, (((1,), (1,)), ((), ())), preferred_element_type=f32).astype(bf16)
    for device in range(64):
        head = device // 8
        served_ref[device] = served[head * 16 : head * 16 + 16]


def attention(
    colour_ref,
    mine_ref,
    one_ref,
    two_ref,
    three_ref,
    gain_ref,
    served_ref,
    pick_ref,
    seg_ref,
    query_weight_ref,
    output_weight_ref,
    own_ref,
    send_one_ref,
    send_two_ref,
    send_three_ref,
    query_weight,
    output_weight,
    context_ref,
    sems,
):
    def start_of(step, size):
        return pl.multiple_of(lax.rem(colour_ref[0] + step, 4) * size, size)

    copies = []
    for step in range(4):
        rows = query_weight_ref.at[pl.ds(start_of(step, D // 4), D // 4)]
        copies.append(pltpu.make_async_copy(rows, query_weight.at[step], sems.at[step]))
    copies.append(pltpu.make_async_copy(output_weight_ref, output_weight, sems.at[4]))
    for copy in copies:
        copy.start()
    query = jnp.zeros((128, HD), f32)
    squares = jnp.zeros((128, 1), f32)
    for step, ref in enumerate((mine_ref, one_ref, two_ref, three_ref)):
        part, more = gained(ref, gain_ref, start_of(step, D // 4))
        squares = squares + more
        copies[step].wait()
        query = query + jnp.dot(part, query_weight[step], preferred_element_type=f32)
    scale = lax.rsqrt(squares / D + eps)
    query = (query * scale).astype(bf16)
    both = jnp.dot(pick_ref[...], served_ref[...], preferred_element_type=f32)
    scale = jnp.broadcast_to(scale, (128, 128)).T
    key_t = (both[:128] * scale).astype(bf16)
    value_t = (both[128:] * scale).astype(bf16)
    scores = jnp.dot(query, key_t, preferred_element_type=f32) * (1.0 / np.sqrt(np.float32(HD)))
    rows = lax.broadcasted_iota(jnp.int32, (128, 128), 0)
    columns = lax.broadcasted_iota(jnp.int32, (128, 128), 1)
    seg = jnp.broadcast_to(seg_ref[...].astype(f32), (128, 128))
    allowed = (rows >= columns) & (seg == seg.T)
    scores = jnp.where(allowed, scores, -1e30)
    weights = jnp.exp(scores - jnp.max(scores, axis=1, keepdims=True))
    weights = (weights / jnp.sum(weights, axis=1, keepdims=True)).astype(bf16)
    context_ref[...] = lax.dot_general(weights, value_t, (((1,), (1,)), ((), ())), preferred_element_type=f32)
    turned = jnp.concatenate([context_ref[pl.ds(start_of(step, 32), 32), :] for step in range(4)], axis=0).astype(bf16)
    copies[4].wait()
    for start in range(0, D, 1024):
        at = pl.ds(start, 1024)
        product = jnp.dot(turned, output_weight[:, at], preferred_element_type=f32)
        own_ref[:, at] = product[:32]
        send_one_ref[:, at] = product[32:64].astype(bf16)
        send_two_ref[:, at] = product[64:96].astype(bf16)
        send_three_ref[:, at] = product[96:].astype(bf16)


def vmem_call(kernel, ins, outs, scratch=(), hbm=0, flops=0):
    vmem = pl.BlockSpec(memory_space=pltpu.VMEM)
    return pl.pallas_call(
        kernel,
        out_shape=[jax.ShapeDtypeStruct(*out) for out in outs],
        in_specs=[pl.BlockSpec(memory_space=pltpu.SMEM)] + [vmem] * ins + [pl.BlockSpec(memory_space=pl.ANY)] * hbm,
        out_specs=[vmem] * len(outs),
        scratch_shapes=list(scratch),
        compiler_params=pltpu.CompilerParams(vmem_limit_bytes=VMEM_MB * 2**20),
        cost_estimate=pl.CostEstimate(flops=flops, bytes_accessed=2**22, transcendentals=0),
        name=kernel.__name__,
    )


def shards(
    tokens,
    sequence_numbers,
    query_projection_weight,
    key_projection_weight,
    value_projection_weight,
    output_projection_weight,
    attention_norm_gain,
    closing_norm_gain,
    projector,
    student_hidden_rows,
    student_norm_gain,
    adapter_down_map,
    adapter_up_map,
):
    tp_index = lax.axis_index(TP)
    colour = lax.rem(lax.axis_index("x") + 2 * lax.axis_index("yl"), 4)

    with jax.named_scope("tokens"):
        quarters = tokens.reshape(2, 4, D // 4).transpose(1, 0, 2)
        by_colour = jnp.stack([quarters, jnp.roll(quarters, -2, axis=0)], axis=1)
        by_colour = jnp.broadcast_to(by_colour[:, None], (4, 8, 2, 2, D // 4)).reshape(64, 2, D // 4)
        by_colour, key_columns, value_columns = lax.optimization_barrier(
            (by_colour, key_projection_weight, value_projection_weight)
        )
        mine = exchange(by_colour, TP).reshape(128, D // 4)
        parts = [mine, from_x(mine, 1), from_yl(mine), from_x(mine, 3)]
        at = lax.rem(tp_index, 16) * HD
        raw_cols = jnp.where(
            lax.axis_index("yl") == 0,
            lax.dynamic_slice_in_dim(parts[0], at, HD, 1),
            lax.dynamic_slice_in_dim(parts[2], at, HD, 1),
        )

    with jax.named_scope("kv_weights"):
        columns = jnp.stack([key_columns.T, value_columns.T]).reshape(2, 2, KV, D)

        def features(step):
            return lax.dynamic_slice_in_dim(columns, lax.rem(colour + step, 4) * (D // 4), D // 4, 3)

        kv = [features(step).reshape(32, D // 4) for step in range(4)]
        kv = [kv[0], from_x(kv[1], 3), from_yl(kv[2]), from_x(kv[3], 1)]
        kv = jnp.stack(kv).reshape(16, KV, D // 4).transpose(1, 0, 2).reshape(128, D // 4)

    with jax.named_scope("own_quarter"):
        gain = attention_norm_gain.reshape(1, D)
        where = colour.reshape(1)
        (served,) = vmem_call(own_quarter, 3, [((64, 16, 128), bf16)], flops=2**31)(where, mine, gain, kv)
        served = exchange(served, TP).reshape(1024, 128)

    with jax.named_scope("attention"):
        total, *sent = vmem_call(
            attention,
            8,
            [((32, D), f32)] + [((32, D), bf16)] * 3,
            scratch=[
                pltpu.VMEM((4, D // 4, HD), bf16),
                pltpu.VMEM((HD, D), bf16),
                pltpu.VMEM((128, HD), f32),
                pltpu.SemaphoreType.DMA((5,)),
            ],
            hbm=2,
            flops=2**31,
        )(
            where,
            *parts,
            gain,
            served,
            jnp.asarray(pick_rows(), bf16),
            sequence_numbers,
            query_projection_weight,
            output_projection_weight,
        )

    with jax.named_scope("output"):
        total = total + from_x(sent[0], 3).astype(f32) + from_yl(sent[1]).astype(f32) + from_x(sent[2], 1).astype(f32)
        columns = total.astype(bf16).reshape(32, 64, HD).transpose(1, 0, 2)
        columns = exchange(columns, TP).reshape(4, 8, 2, 32, HD)
        columns = jnp.sum(columns.astype(f32), axis=1)
        summed = (columns[:, 0] + jnp.roll(columns[:, 1], 2, axis=0)).reshape(128, HD)
        resid = raw_cols.astype(f32) + summed

    with jax.named_scope("target"):
        squares = jnp.sum(resid * resid, axis=1)
        high = squares.astype(bf16)
        low = (squares - high.astype(f32)).astype(bf16)
        gain_cols = lax.dynamic_slice_in_dim(closing_norm_gain, tp_index * HD, HD, 0)
        features = (resid * gain_cols).astype(bf16)
        projected = jnp.dot(features, projector, preferred_element_type=f32).astype(bf16)
        tail = jnp.pad(jnp.stack([high, low], axis=1), ((0, 0), (0, 126)))
        rows_out = jnp.concatenate([projected, tail], axis=1).reshape(64, 2, WIDTH + 128)
        rows_in = jnp.sum(exchange(rows_out, TP).astype(f32), axis=0)
        squares = rows_in[:, WIDTH] + rows_in[:, WIDTH + 1]
        target = rows_in[:, :WIDTH] * lax.rsqrt(squares / D + eps)[:, None]

    with jax.named_scope("student"):
        student = student_hidden_rows.astype(f32)
        student_normed = rms_norm(student, student_norm_gain).astype(bf16)
        lowrank = jnp.dot(student_normed, adapter_down_map, preferred_element_type=f32).astype(bf16)
        reached = student + jnp.dot(lowrank, adapter_up_map, preferred_element_type=f32)
        diff = reached - target
        token_loss = jnp.mean(diff * diff, axis=1)
        scaled = diff / jnp.sqrt(f32(512))
        back = lax.dot_general(
            scaled, adapter_up_map.astype(f32), (((1,), (1,)), ((), ())), precision=highest, preferred_element_type=f32
        )

    with jax.named_scope("columns"):

        def groups(v):
            return v.reshape(2, 28, 128).transpose(1, 0, 2)

        right = jnp.concatenate([back.astype(bf16), lowrank], axis=1)
        message = jnp.concatenate(
            [
                jnp.pad(jnp.concatenate([groups(student_normed), groups(scaled.astype(bf16))], axis=2), ((0, 4), (0, 0), (0, 0))),
                jnp.broadcast_to(right, (32, 2, 128)),
            ],
            axis=2,
        )
        message = jnp.broadcast_to(message[:, None], (32, 8, 2, 384)).reshape(256, 2, 384)
        message = exchange(message, WIDE + ("z",)).reshape(512, 384)

        def product(left, right):
            return lax.dot_general(left, right, (((0,), (0,)), ((), ())), preferred_element_type=f32)

        down = product(message[:, 256:320], message[:, :128])
        up = product(message[:, 320:], message[:, 128:256])
        chunk = jnp.concatenate([down, up], axis=0).astype(bf16)

    with jax.named_scope("gradients"):
        whole = exchange(jnp.broadcast_to(chunk, (32, 128, 128)), WIDE)[:28].astype(f32)
        grad_down = whole[:, :64].transpose(0, 2, 1).reshape(WIDTH, RANK)
        grad_up = whole[:, 64:].transpose(1, 0, 2).reshape(RANK, WIDTH)
    return (token_loss, grad_down, grad_up)


def solution(mesh):
    fine = Mesh(np.asarray(mesh.devices).reshape(2, 2, 4, 8, 2), ALL)
    return jax.shard_map(
        shards,
        mesh=fine,
        in_specs=(
            P(ALL, None),
            P(("yh", "core"), None),
            P(None, TP),
            P(None, TP),
            P(None, TP),
            P(TP, None),
            P(),
            P(),
            P(TP, None),
            P(ALL, None),
            P(),
            P(),
            P(),
        ),
        out_specs=(P(ALL), P(), P()),
        check_vma=False,
    )
```

```python
import jax
import jax.numpy as jnp
import numpy as np
from jax import lax
from jax.experimental import pallas as pl
from jax.experimental.pallas import tpu as pltpu
from jax.sharding import Mesh
from jax.sharding import PartitionSpec as P

D = 8192
H = 64
KV = 8
HD = 128
WIDTH = 3584
RANK = 64
TP = ("x", "z", "yl")
ALL = ("yh", "core", "x", "z", "yl")
WIDE = ("yh", "core", "x", "yl")

eps = 1e-06
VMEM_MB = 24
f32 = jnp.float32
bf16 = jnp.bfloat16
highest = lax.Precision.HIGHEST


def rms_norm(values, gain):
    mean_sq = jnp.mean(values * values, axis=-1, keepdims=True)
    return values * lax.rsqrt(mean_sq + eps) * gain


def exchange(blocks, axes):
    return lax.all_to_all(blocks, axes, split_axis=0, concat_axis=0, tiled=True)


def from_x(block, step):
    return lax.ppermute(block, "x", [((i + step) % 4, i) for i in range(4)])


def from_z(block, step):
    return lax.ppermute(block, "z", [((i + step) % 8, i) for i in range(8)])


def from_yl(block):
    return lax.ppermute(block, "yl", [(0, 1), (1, 0)])


def pick_rows():
    pick = np.zeros((2, 4, 8, 2, 2, 4, 8, 2, 4, 2, 2), np.float32)
    for x in range(4):
        for yl in range(2):
            for step, (sx, syl) in enumerate([(x, yl), ((x + 1) % 4, yl), (x, 1 - yl), ((x + 3) % 4, yl)]):
                for z in range(8):
                    for part in range(2):
                        for e in range(2):
                            pick[part, x, z, yl, e, sx, z, syl, step, part, e] = 1
    return pick.reshape(256, 1024)


def gained(part_ref, gain_ref, start):
    wide = part_ref[...].astype(f32)
    squares = jnp.sum(wide * wide, axis=1, keepdims=True)
    return (wide * gain_ref[:, pl.ds(start, D // 4)]).astype(bf16), squares


def own_quarter(colour_ref, mine_ref, gain_ref, kv_ref, served_ref):
    part, _ = gained(mine_ref, gain_ref, pl.multiple_of(colour_ref[0] * (D // 4), D // 4))
    served = lax.dot_general(kv_ref[...], part, (((1,), (1,)), ((), ())), preferred_element_type=f32).astype(bf16)
    for device in range(64):
        head = device // 8
        served_ref[device] = served[head * 16 : head * 16 + 16]


def attention(
    colour_ref,
    mine_ref,
    one_ref,
    two_ref,
    three_ref,
    gain_ref,
    served_ref,
    pick_ref,
    seg_ref,
    query_weight_ref,
    output_weight_ref,
    own_ref,
    send_one_ref,
    send_two_ref,
    send_three_ref,
    query_weight,
    output_weight,
    context_ref,
    sems,
):
    def start_of(step, size):
        return pl.multiple_of(lax.rem(colour_ref[0] + step, 4) * size, size)

    copies = []
    for step in range(4):
        rows = query_weight_ref.at[pl.ds(start_of(step, D // 4), D // 4)]
        copies.append(pltpu.make_async_copy(rows, query_weight.at[step], sems.at[step]))
    copies.append(pltpu.make_async_copy(output_weight_ref, output_weight, sems.at[4]))
    for copy in copies:
        copy.start()
    query = jnp.zeros((128, HD), f32)
    squares = jnp.zeros((128, 1), f32)
    for step, ref in enumerate((mine_ref, one_ref, two_ref, three_ref)):
        part, more = gained(ref, gain_ref, start_of(step, D // 4))
        squares = squares + more
        copies[step].wait()
        query = query + jnp.dot(part, query_weight[step], preferred_element_type=f32)
    scale = lax.rsqrt(squares / D + eps)
    query = (query * scale).astype(bf16)
    both = jnp.dot(pick_ref[...], served_ref[...], preferred_element_type=f32)
    scale = jnp.broadcast_to(scale, (128, 128)).T
    key_t = (both[:128] * scale).astype(bf16)
    value_t = (both[128:] * scale).astype(bf16)
    scores = jnp.dot(query, key_t, preferred_element_type=f32) * (1.0 / np.sqrt(np.float32(HD)))
    rows = lax.broadcasted_iota(jnp.int32, (128, 128), 0)
    columns = lax.broadcasted_iota(jnp.int32, (128, 128), 1)
    seg = jnp.broadcast_to(seg_ref[...].astype(f32), (128, 128))
    allowed = (rows >= columns) & (seg == seg.T)
    scores = jnp.where(allowed, scores, -1e30)
    weights = jnp.exp(scores - jnp.max(scores, axis=1, keepdims=True))
    weights = (weights / jnp.sum(weights, axis=1, keepdims=True)).astype(bf16)
    context_ref[...] = lax.dot_general(weights, value_t, (((1,), (1,)), ((), ())), preferred_element_type=f32)
    turned = jnp.concatenate([context_ref[pl.ds(start_of(step, 32), 32), :] for step in range(4)], axis=0).astype(bf16)
    copies[4].wait()
    for start in range(0, D, 1024):
        at = pl.ds(start, 1024)
        product = jnp.dot(turned, output_weight[:, at], preferred_element_type=f32)
        own_ref[:, at] = product[:32]
        send_one_ref[:, at] = product[32:64].astype(bf16)
        send_two_ref[:, at] = product[64:96].astype(bf16)
        send_three_ref[:, at] = product[96:].astype(bf16)


def project(
    colour_ref, columns_ref, raw_ref, gain_ref, projector_ref, own_ref, send_one_ref, send_two_ref, send_three_ref
):
    sums = []
    for x in range(4):
        for yl in range(2):
            part = jnp.zeros((32, HD), f32)
            for z in range(8):
                part = part + columns_ref[x * 16 + z * 2 + yl].astype(f32)
            sums.append(part)
    summed = jnp.concatenate([sums[2 * c] + sums[2 * ((c + 2) % 4) + 1] for c in range(4)], axis=0)
    resid = raw_ref[...].astype(f32) + summed
    squares = jnp.sum(resid * resid, axis=1, keepdims=True)
    high = squares.astype(bf16)
    low = (squares - high.astype(f32)).astype(bf16)
    lane = lax.broadcasted_iota(jnp.int32, (128, 128), 1)
    tail = jnp.where(lane == 0, high.astype(f32), jnp.where(lane == 1, low.astype(f32), 0.0)).astype(bf16)
    features = (resid * gain_ref[...]).astype(bf16)
    row = lax.broadcasted_iota(jnp.int32, (128, 128), 0)
    yl = (row >> 4) & 1
    x = (colour_ref[0] + (row >> 5) + 2 * yl) & 3
    token = 32 * x + 4 * ((row >> 1) & 7) + 2 * yl + (row & 1)
    order = jnp.where(lane == token, 1.0, 0.0).astype(bf16)
    features = jnp.dot(order, features, preferred_element_type=f32).astype(bf16)
    tail = jnp.dot(order, tail, preferred_element_type=f32)
    for start in range(0, WIDTH + 128, 512):
        at = pl.ds(start, min(512, WIDTH + 128 - start))
        product = tail if start == WIDTH else jnp.dot(features, projector_ref[:, at], preferred_element_type=f32)
        own_ref[:, at] = product[:32]
        send_one_ref[:, at] = product[32:64].astype(bf16)
        send_two_ref[:, at] = product[64:96].astype(bf16)
        send_three_ref[:, at] = product[96:].astype(bf16)


def same_colour():
    def index(x, z, yl):
        return x * 16 + z * 2 + yl

    return [
        [index(c, z, 0) for z in range(8)] + [index((c + 2) % 4, z, 1) for z in range(8)] for c in range(4)
    ]


def same_quarter():
    return [[c * 8 + quarter + 4 * half for c in range(32) for half in range(2)] for quarter in range(4)]


def spread(tokens_ref, out_ref):
    for colour in range(4):
        block = tokens_ref[:, colour * (D // 4) : (colour + 1) * (D // 4)]
        for z in range(8):
            for yl in range(2):
                out_ref[(colour + 2 * yl) % 4 * 16 + z * 2 + yl] = block


def vmem_call(kernel, ins, outs, scratch=(), hbm=0, flops=0):
    vmem = pl.BlockSpec(memory_space=pltpu.VMEM)
    return pl.pallas_call(
        kernel,
        out_shape=[jax.ShapeDtypeStruct(*out) for out in outs],
        in_specs=[pl.BlockSpec(memory_space=pltpu.SMEM)] + [vmem] * ins + [pl.BlockSpec(memory_space=pl.ANY)] * hbm,
        out_specs=[vmem] * len(outs),
        scratch_shapes=list(scratch),
        compiler_params=pltpu.CompilerParams(vmem_limit_bytes=VMEM_MB * 2**20),
        cost_estimate=pl.CostEstimate(flops=flops, bytes_accessed=2**22, transcendentals=0),
        name=kernel.__name__,
    )


def shards(
    tokens,
    sequence_numbers,
    query_projection_weight,
    key_projection_weight,
    value_projection_weight,
    output_projection_weight,
    attention_norm_gain,
    closing_norm_gain,
    projector,
    student_hidden_rows,
    student_norm_gain,
    adapter_down_map,
    adapter_up_map,
):
    tp_index = lax.axis_index(TP)
    colour = lax.rem(lax.axis_index("x") + 2 * lax.axis_index("yl"), 4)

    with jax.named_scope("tokens"):
        (by_colour,) = pl.pallas_call(
            spread,
            out_shape=[jax.ShapeDtypeStruct((64, 2, D // 4), bf16)],
            in_specs=[pl.BlockSpec(memory_space=pltpu.VMEM)],
            out_specs=[pl.BlockSpec(memory_space=pltpu.VMEM)],
            compiler_params=pltpu.CompilerParams(vmem_limit_bytes=VMEM_MB * 2**20),
        )(tokens)
        by_colour, key_columns, value_columns = lax.optimization_barrier(
            (by_colour, key_projection_weight, value_projection_weight)
        )
        mine = exchange(by_colour, TP).reshape(128, D // 4)
        parts = [mine, from_x(mine, 1), from_yl(mine), from_x(mine, 3)]
        at = lax.rem(tp_index, 16) * HD
        raw_cols = jnp.where(
            lax.axis_index("yl") == 0,
            lax.dynamic_slice_in_dim(parts[0], at, HD, 1),
            lax.dynamic_slice_in_dim(parts[2], at, HD, 1),
        )

    with jax.named_scope("kv_weights"):
        columns = jnp.stack([key_columns.T, value_columns.T]).reshape(2, 2, KV, D)

        def features(step):
            return lax.dynamic_slice_in_dim(columns, lax.rem(colour + step, 4) * (D // 4), D // 4, 3)

        kv = [features(step).reshape(32, D // 4) for step in range(4)]
        kv = [kv[0], from_x(kv[1], 3), from_yl(kv[2]), from_x(kv[3], 1)]
        kv = jnp.stack(kv).reshape(16, KV, D // 4).transpose(1, 0, 2).reshape(128, D // 4)

    with jax.named_scope("own_quarter"):
        gain = attention_norm_gain.reshape(1, D)
        where = colour.reshape(1)
        (served,) = vmem_call(own_quarter, 3, [((64, 16, 128), bf16)], flops=2**31)(where, mine, gain, kv)
        served = exchange(served, TP).reshape(1024, 128)

    with jax.named_scope("attention"):
        total, *sent = vmem_call(
            attention,
            8,
            [((32, D), f32)] + [((32, D), bf16)] * 3,
            scratch=[
                pltpu.VMEM((4, D // 4, HD), bf16),
                pltpu.VMEM((HD, D), bf16),
                pltpu.VMEM((128, HD), f32),
                pltpu.SemaphoreType.DMA((5,)),
            ],
            hbm=2,
            flops=2**31,
        )(
            where,
            *parts,
            gain,
            served,
            jnp.asarray(pick_rows(), bf16),
            sequence_numbers,
            query_projection_weight,
            output_projection_weight,
        )

    with jax.named_scope("output"):
        total = total + from_x(sent[0], 3).astype(f32) + from_yl(sent[1]).astype(f32) + from_x(sent[2], 1).astype(f32)
        columns = total.astype(bf16).reshape(32, 64, HD).transpose(1, 0, 2)
        columns = exchange(columns, TP)

    with jax.named_scope("target"):
        gain_cols = lax.dynamic_slice_in_dim(closing_norm_gain, tp_index * HD, HD, 0).reshape(1, HD)
        total, *sent = vmem_call(
            project, 4, [((32, WIDTH + 128), f32)] + [((32, WIDTH + 128), bf16)] * 3, flops=2**31
        )(where, columns, raw_cols, gain_cols, projector)
        total = total + from_x(sent[0], 3).astype(f32) + from_yl(sent[1]).astype(f32) + from_x(sent[2], 1).astype(f32)
        squares = total[:, WIDTH] + total[:, WIDTH + 1]
        high = squares.astype(bf16)
        low = (squares - high.astype(f32)).astype(bf16)
        tail = jnp.pad(jnp.stack([high, low], axis=1), ((0, 0), (0, 126)))
        rows_out = jnp.concatenate([total[:, :WIDTH].astype(bf16), tail], axis=1).reshape(16, 2, WIDTH + 128)
        rows_in = lax.all_to_all(rows_out, TP, split_axis=0, concat_axis=0, axis_index_groups=same_colour(), tiled=True)
        rows_in = jnp.sum(rows_in.astype(f32), axis=0)
        squares = rows_in[:, WIDTH] + rows_in[:, WIDTH + 1]
        target = rows_in[:, :WIDTH] * lax.rsqrt(squares / D + eps)[:, None]

    with jax.named_scope("student"):
        student = student_hidden_rows.astype(f32)
        student_normed = rms_norm(student, student_norm_gain).astype(bf16)
        lowrank = jnp.dot(student_normed, adapter_down_map, preferred_element_type=f32).astype(bf16)
        reached = student + jnp.dot(lowrank, adapter_up_map, preferred_element_type=f32)
        diff = reached - target
        token_loss = jnp.mean(diff * diff, axis=1)
        scaled = diff / jnp.sqrt(f32(512))
        back = lax.dot_general(
            scaled, adapter_up_map.astype(f32), (((1,), (1,)), ((), ())), precision=highest, preferred_element_type=f32
        )

    with jax.named_scope("columns"):

        def groups(v):
            return v.reshape(2, 28, 128).transpose(1, 0, 2)

        right = jnp.concatenate([back.astype(bf16), lowrank], axis=1)
        message = jnp.concatenate(
            [
                jnp.pad(jnp.concatenate([groups(student_normed), groups(scaled.astype(bf16))], axis=2), ((0, 4), (0, 0), (0, 0))),
                jnp.broadcast_to(right, (32, 2, 128)),
            ],
            axis=2,
        )
        message = jnp.broadcast_to(message[:, None], (32, 2, 2, 384)).reshape(64, 2, 384)
        message = lax.all_to_all(
            message, WIDE + ("z",), split_axis=0, concat_axis=0, axis_index_groups=same_quarter(), tiled=True
        ).reshape(128, 384)

        def product(left, right):
            return lax.dot_general(left, right, (((0,), (0,)), ((), ())), preferred_element_type=f32)

        down = product(message[:, 256:320], message[:, :128])
        up = product(message[:, 320:], message[:, 128:256])
        part = jnp.concatenate([down, up], axis=0).astype(bf16)
        one, two, three = (from_z(part, step).astype(f32) for step in (1, 2, 7))
        chunk = ((part.astype(f32) + two) + (one + three)).astype(bf16)

    with jax.named_scope("gradients"):
        whole = exchange(jnp.broadcast_to(chunk, (32, 128, 128)), WIDE)[:28].astype(f32)
        grad_down = whole[:, :64].transpose(0, 2, 1).reshape(WIDTH, RANK)
        grad_up = whole[:, 64:].transpose(1, 0, 2).reshape(RANK, WIDTH)
    return (token_loss, grad_down, grad_up)


def solution(mesh):
    fine = Mesh(np.asarray(mesh.devices).reshape(2, 2, 4, 8, 2), ALL)
    return jax.shard_map(
        shards,
        mesh=fine,
        in_specs=(
            P(ALL, None),
            P(("yh", "core"), None),
            P(None, TP),
            P(None, TP),
            P(None, TP),
            P(TP, None),
            P(),
            P(),
            P(TP, None),
            P(ALL, None),
            P(),
            P(),
            P(),
        ),
        out_specs=(P(ALL), P(), P()),
        check_vma=False,
    )
```

```python
import jax
import jax.numpy as jnp
import numpy as np
from jax import lax
from jax.experimental import pallas as pl
from jax.experimental.pallas import tpu as pltpu
from jax.sharding import Mesh
from jax.sharding import PartitionSpec as P

D = 8192
H = 64
KV = 8
HD = 128
WIDTH = 3584
RANK = 64
TP = ("x", "z", "yl")
ALL = ("yh", "core", "x", "z", "yl")
WIDE = ("yh", "core", "x", "yl")

eps = 1e-06
VMEM_MB = 24
f32 = jnp.float32
bf16 = jnp.bfloat16
highest = lax.Precision.HIGHEST


def rms_norm(values, gain):
    mean_sq = jnp.mean(values * values, axis=-1, keepdims=True)
    return values * lax.rsqrt(mean_sq + eps) * gain


def exchange(blocks, axes):
    return lax.all_to_all(blocks, axes, split_axis=0, concat_axis=0, tiled=True)


def from_x(block, step):
    return lax.ppermute(block, "x", [((i + step) % 4, i) for i in range(4)])


def from_z(block, step):
    return lax.ppermute(block, "z", [((i + step) % 8, i) for i in range(8)])


def from_yl(block):
    return lax.ppermute(block, "yl", [(0, 1), (1, 0)])


def pick_rows():
    pick = np.zeros((2, 4, 8, 2, 2, 4, 8, 2, 4, 2, 2), np.float32)
    for x in range(4):
        for yl in range(2):
            for step, (sx, syl) in enumerate([(x, yl), ((x + 1) % 4, yl), (x, 1 - yl), ((x + 3) % 4, yl)]):
                for z in range(8):
                    for part in range(2):
                        for e in range(2):
                            pick[part, x, z, yl, e, sx, z, syl, step, part, e] = 1
    return pick.reshape(256, 1024)


def gained(part_ref, gain_ref, start):
    wide = part_ref[...].astype(f32)
    squares = jnp.sum(wide * wide, axis=1, keepdims=True)
    return (wide * gain_ref[:, pl.ds(start, D // 4)]).astype(bf16), squares


def own_quarter(colour_ref, mine_ref, gain_ref, kv_ref, served_ref):
    part, _ = gained(mine_ref, gain_ref, pl.multiple_of(colour_ref[0] * (D // 4), D // 4))
    served = lax.dot_general(kv_ref[...], part, (((1,), (1,)), ((), ())), preferred_element_type=f32).astype(bf16)
    for device in range(64):
        head = device // 8
        served_ref[device] = served[head * 16 : head * 16 + 16]


def attention(
    colour_ref,
    mine_ref,
    one_ref,
    two_ref,
    three_ref,
    gain_ref,
    served_ref,
    pick_ref,
    seg_ref,
    query_weight_ref,
    output_weight_ref,
    own_ref,
    send_one_ref,
    send_two_ref,
    send_three_ref,
):
    def start_of(step):
        return pl.multiple_of(lax.rem(colour_ref[0] + step, 4) * (D // 4), D // 4)

    query = jnp.zeros((128, HD), f32)
    squares = jnp.zeros((128, 1), f32)
    for step, ref in enumerate((mine_ref, one_ref, two_ref, three_ref)):
        part, more = gained(ref, gain_ref, start_of(step))
        squares = squares + more
        rows = query_weight_ref[pl.ds(start_of(step), D // 4), :]
        query = query + jnp.dot(part, rows, preferred_element_type=f32)
    scale = lax.rsqrt(squares / D + eps)
    query = (query * scale).astype(bf16)
    both = jnp.dot(pick_ref[...], served_ref[...], preferred_element_type=f32)
    scale = jnp.broadcast_to(scale, (128, 128)).T
    key_t = (both[:128] * scale).astype(bf16)
    value_t = (both[128:] * scale).astype(bf16)
    scores = jnp.dot(query, key_t, preferred_element_type=f32) * (1.0 / np.sqrt(np.float32(HD)))
    rows = lax.broadcasted_iota(jnp.int32, (128, 128), 0)
    columns = lax.broadcasted_iota(jnp.int32, (128, 128), 1)
    seg = jnp.broadcast_to(seg_ref[...].astype(f32), (128, 128))
    allowed = (rows >= columns) & (seg == seg.T)
    scores = jnp.where(allowed, scores, -1e30)
    weights = jnp.exp(scores - jnp.max(scores, axis=1, keepdims=True))
    weights = (weights / jnp.sum(weights, axis=1, keepdims=True)).astype(bf16)
    context = lax.dot_general(weights, value_t, (((1,), (1,)), ((), ())), preferred_element_type=f32).astype(bf16)
    refs = (own_ref, send_one_ref, send_two_ref, send_three_ref)
    for step in range(4):
        for z in range(8):
            at = pl.multiple_of(start_of(step) + z * 256, 256)
            product = jnp.dot(context, output_weight_ref[:, pl.ds(at, 256)], preferred_element_type=f32)
            for yl in range(2):
                ref = refs[(step + 2 * yl) % 4]
                ref[yl * 8 + z] = product[:, yl * 128 : yl * 128 + 128].astype(ref.dtype)


def project(
    colour_ref, columns_ref, raw_ref, gain_ref, projector_ref, own_ref, send_one_ref, send_two_ref, send_three_ref
):
    summed = jnp.zeros((128, HD), f32)
    for device in range(16):
        summed = summed + columns_ref[device].astype(f32)
    resid = raw_ref[...].astype(f32) + summed
    squares = jnp.sum(resid * resid, axis=1, keepdims=True)
    high = squares.astype(bf16)
    low = (squares - high.astype(f32)).astype(bf16)
    lane = lax.broadcasted_iota(jnp.int32, (128, 128), 1)
    tail = jnp.where(lane == 0, high.astype(f32), jnp.where(lane == 1, low.astype(f32), 0.0)).astype(bf16)
    features = (resid * gain_ref[...]).astype(bf16)
    row = lax.broadcasted_iota(jnp.int32, (128, 128), 0)
    yl = (row >> 4) & 1
    x = (colour_ref[0] + (row >> 5) + 2 * yl) & 3
    token = 32 * x + 4 * ((row >> 1) & 7) + 2 * yl + (row & 1)
    order = jnp.where(lane == token, 1.0, 0.0).astype(bf16)
    features = jnp.dot(order, features, preferred_element_type=f32).astype(bf16)
    tail = jnp.dot(order, tail, preferred_element_type=f32)
    for start in range(0, WIDTH + 128, 512):
        at = pl.ds(start, min(512, WIDTH + 128 - start))
        product = tail if start == WIDTH else jnp.dot(features, projector_ref[:, at], preferred_element_type=f32)
        own_ref[:, at] = product[:32]
        send_one_ref[:, at] = product[32:64].astype(bf16)
        send_two_ref[:, at] = product[64:96].astype(bf16)
        send_three_ref[:, at] = product[96:].astype(bf16)


def same_colour():
    def index(x, z, yl):
        return x * 16 + z * 2 + yl

    return [
        [index(c, z, 0) for z in range(8)] + [index((c + 2) % 4, z, 1) for z in range(8)] for c in range(4)
    ]


def same_quarter():
    return [[c * 8 + quarter + 4 * half for c in range(32) for half in range(2)] for quarter in range(4)]


def spread(tokens_ref, out_ref):
    for colour in range(4):
        block = tokens_ref[:, colour * (D // 4) : (colour + 1) * (D // 4)]
        for z in range(8):
            for yl in range(2):
                out_ref[(colour + 2 * yl) % 4 * 16 + z * 2 + yl] = block


def vmem_call(kernel, ins, outs, flops):
    vmem = pl.BlockSpec(memory_space=pltpu.VMEM)
    return pl.pallas_call(
        kernel,
        out_shape=[jax.ShapeDtypeStruct(*out) for out in outs],
        in_specs=[pl.BlockSpec(memory_space=pltpu.SMEM)] + [vmem] * ins,
        out_specs=[vmem] * len(outs),
        compiler_params=pltpu.CompilerParams(vmem_limit_bytes=VMEM_MB * 2**20),
        cost_estimate=pl.CostEstimate(flops=flops, bytes_accessed=2**22, transcendentals=0),
        name=kernel.__name__,
    )


def shards(
    tokens,
    sequence_numbers,
    query_projection_weight,
    key_projection_weight,
    value_projection_weight,
    output_projection_weight,
    attention_norm_gain,
    closing_norm_gain,
    projector,
    student_hidden_rows,
    student_norm_gain,
    adapter_down_map,
    adapter_up_map,
):
    tp_index = lax.axis_index(TP)
    colour = lax.rem(lax.axis_index("x") + 2 * lax.axis_index("yl"), 4)

    with jax.named_scope("tokens"):
        (by_colour,) = pl.pallas_call(
            spread,
            out_shape=[jax.ShapeDtypeStruct((64, 2, D // 4), bf16)],
            in_specs=[pl.BlockSpec(memory_space=pltpu.VMEM)],
            out_specs=[pl.BlockSpec(memory_space=pltpu.VMEM)],
            compiler_params=pltpu.CompilerParams(vmem_limit_bytes=VMEM_MB * 2**20),
        )(tokens)
        by_colour, key_columns, value_columns = lax.optimization_barrier(
            (by_colour, key_projection_weight, value_projection_weight)
        )
        mine = exchange(by_colour, TP).reshape(128, D // 4)
        parts = [mine, from_x(mine, 1), from_yl(mine), from_x(mine, 3)]
        at = lax.rem(tp_index, 16) * HD
        raw_cols = jnp.where(
            lax.axis_index("yl") == 0,
            lax.dynamic_slice_in_dim(parts[0], at, HD, 1),
            lax.dynamic_slice_in_dim(parts[2], at, HD, 1),
        )

    with jax.named_scope("kv_weights"):
        columns = jnp.stack([key_columns.T, value_columns.T]).reshape(2, 2, KV, D)

        def features(step):
            return lax.dynamic_slice_in_dim(columns, lax.rem(colour + step, 4) * (D // 4), D // 4, 3)

        kv = [features(step).reshape(32, D // 4) for step in range(4)]
        kv = [kv[0], from_x(kv[1], 3), from_yl(kv[2]), from_x(kv[3], 1)]
        kv = jnp.stack(kv).reshape(16, KV, D // 4).transpose(1, 0, 2).reshape(128, D // 4)

    with jax.named_scope("own_quarter"):
        gain = attention_norm_gain.reshape(1, D)
        where = colour.reshape(1)
        (served,) = vmem_call(own_quarter, 3, [((64, 16, 128), bf16)], flops=2**31)(where, mine, gain, kv)
        served = exchange(served, TP).reshape(1024, 128)

    with jax.named_scope("attention"):
        block = (16, 128, HD)
        total, *sent = vmem_call(attention, 10, [(block, f32)] + [(block, bf16)] * 3, flops=2**31)(
            where,
            *parts,
            gain,
            served,
            jnp.asarray(pick_rows(), bf16),
            sequence_numbers,
            query_projection_weight,
            output_projection_weight,
        )

    with jax.named_scope("output"):
        total = total + from_x(sent[0], 3).astype(f32) + from_yl(sent[1]).astype(f32) + from_x(sent[2], 1).astype(f32)
        columns = lax.all_to_all(
            total.astype(bf16), TP, split_axis=0, concat_axis=0, axis_index_groups=same_colour(), tiled=True
        )

    with jax.named_scope("target"):
        gain_cols = lax.dynamic_slice_in_dim(closing_norm_gain, tp_index * HD, HD, 0).reshape(1, HD)
        total, *sent = vmem_call(
            project, 4, [((32, WIDTH + 128), f32)] + [((32, WIDTH + 128), bf16)] * 3, flops=2**31
        )(where, columns, raw_cols, gain_cols, projector)
        total = total + from_x(sent[0], 3).astype(f32) + from_yl(sent[1]).astype(f32) + from_x(sent[2], 1).astype(f32)
        squares = total[:, WIDTH] + total[:, WIDTH + 1]
        high = squares.astype(bf16)
        low = (squares - high.astype(f32)).astype(bf16)
        tail = jnp.pad(jnp.stack([high, low], axis=1), ((0, 0), (0, 126)))
        rows_out = jnp.concatenate([total[:, :WIDTH].astype(bf16), tail], axis=1).reshape(16, 2, WIDTH + 128)
        rows_in = lax.all_to_all(rows_out, TP, split_axis=0, concat_axis=0, axis_index_groups=same_colour(), tiled=True)
        rows_in = jnp.sum(rows_in.astype(f32), axis=0)
        squares = rows_in[:, WIDTH] + rows_in[:, WIDTH + 1]
        target = rows_in[:, :WIDTH] * lax.rsqrt(squares / D + eps)[:, None]

    with jax.named_scope("student"):
        student = student_hidden_rows.astype(f32)
        student_normed = rms_norm(student, student_norm_gain).astype(bf16)
        lowrank = jnp.dot(student_normed, adapter_down_map, preferred_element_type=f32).astype(bf16)
        reached = student + jnp.dot(lowrank, adapter_up_map, preferred_element_type=f32)
        diff = reached - target
        token_loss = jnp.mean(diff * diff, axis=1)
        scaled = diff / jnp.sqrt(f32(512))
        back = lax.dot_general(
            scaled, adapter_up_map.astype(f32), (((1,), (1,)), ((), ())), precision=highest, preferred_element_type=f32
        )

    with jax.named_scope("columns"):

        def groups(v):
            return v.reshape(2, 28, 128).transpose(1, 0, 2)

        right = jnp.concatenate([back.astype(bf16), lowrank], axis=1)
        message = jnp.concatenate(
            [
                jnp.pad(jnp.concatenate([groups(student_normed), groups(scaled.astype(bf16))], axis=2), ((0, 4), (0, 0), (0, 0))),
                jnp.broadcast_to(right, (32, 2, 128)),
            ],
            axis=2,
        )
        message = jnp.broadcast_to(message[:, None], (32, 2, 2, 384)).reshape(64, 2, 384)
        message = lax.all_to_all(
            message, WIDE + ("z",), split_axis=0, concat_axis=0, axis_index_groups=same_quarter(), tiled=True
        ).reshape(128, 384)

        def product(left, right):
            return lax.dot_general(left, right, (((0,), (0,)), ((), ())), preferred_element_type=f32)

        down = product(message[:, 256:320], message[:, :128])
        up = product(message[:, 320:], message[:, 128:256])
        part = jnp.concatenate([down, up], axis=0).astype(bf16)
        one, two, three = (from_z(part, step).astype(f32) for step in (1, 2, 7))
        chunk = ((part.astype(f32) + two) + (one + three)).astype(bf16)

    with jax.named_scope("gradients"):
        whole = exchange(jnp.broadcast_to(chunk, (32, 128, 128)), WIDE)[:28].astype(f32)
        grad_down = whole[:, :64].transpose(0, 2, 1).reshape(WIDTH, RANK)
        grad_up = whole[:, 64:].transpose(1, 0, 2).reshape(RANK, WIDTH)
    return (token_loss, grad_down, grad_up)


def solution(mesh):
    fine = Mesh(np.asarray(mesh.devices).reshape(2, 2, 4, 8, 2), ALL)
    return jax.shard_map(
        shards,
        mesh=fine,
        in_specs=(
            P(ALL, None),
            P(("yh", "core"), None),
            P(None, TP),
            P(None, TP),
            P(None, TP),
            P(TP, None),
            P(),
            P(),
            P(TP, None),
            P(ALL, None),
            P(),
            P(),
            P(),
        ),
        out_specs=(P(ALL), P(), P()),
        check_vma=False,
    )
```

```python
import jax
import jax.numpy as jnp
import numpy as np
from jax import lax
from jax.experimental import pallas as pl
from jax.experimental.pallas import tpu as pltpu
from jax.sharding import Mesh
from jax.sharding import PartitionSpec as P

D = 8192
H = 64
KV = 8
HD = 128
WIDTH = 3584
RANK = 64
TP = ("x", "z", "yl")
ALL = ("yh", "core", "x", "z", "yl")
WIDE = ("yh", "core", "x", "yl")

eps = 1e-06
VMEM_MB = 24
f32 = jnp.float32
bf16 = jnp.bfloat16
highest = lax.Precision.HIGHEST


def rms_norm(values, gain):
    mean_sq = jnp.mean(values * values, axis=-1, keepdims=True)
    return values * lax.rsqrt(mean_sq + eps) * gain


def exchange(blocks, axes):
    return lax.all_to_all(blocks, axes, split_axis=0, concat_axis=0, tiled=True)


def from_x(block, step):
    return lax.ppermute(block, "x", [((i + step) % 4, i) for i in range(4)])


def from_z(block, step):
    return lax.ppermute(block, "z", [((i + step) % 8, i) for i in range(8)])


def from_yl(block):
    return lax.ppermute(block, "yl", [(0, 1), (1, 0)])


def pick_rows():
    pick = np.zeros((2, 4, 8, 2, 2, 4, 8, 2, 4, 2, 2), np.float32)
    for x in range(4):
        for yl in range(2):
            for step, (sx, syl) in enumerate([(x, yl), ((x + 1) % 4, yl), (x, 1 - yl), ((x + 3) % 4, yl)]):
                for z in range(8):
                    for part in range(2):
                        for e in range(2):
                            pick[part, x, z, yl, e, sx, z, syl, step, part, e] = 1
    return pick.reshape(256, 1024)


def gained(part_ref, gain_ref, start):
    wide = part_ref[...].astype(f32)
    squares = jnp.sum(wide * wide, axis=1, keepdims=True)
    return (wide * gain_ref[:, pl.ds(start, D // 4)]).astype(bf16), squares


def own_quarter(colour_ref, mine_ref, gain_ref, kv_ref, served_ref):
    part, _ = gained(mine_ref, gain_ref, pl.multiple_of(colour_ref[0] * (D // 4), D // 4))
    served = lax.dot_general(kv_ref[...], part, (((1,), (1,)), ((), ())), preferred_element_type=f32).astype(bf16)
    for device in range(64):
        head = device // 8
        served_ref[device] = served[head * 16 : head * 16 + 16]


def attention(
    colour_ref,
    mine_ref,
    one_ref,
    two_ref,
    three_ref,
    gain_ref,
    served_ref,
    pick_ref,
    seg_ref,
    query_weight_ref,
    output_weight_ref,
    own_ref,
    send_one_ref,
    send_two_ref,
    send_three_ref,
):
    def start_of(step):
        return pl.multiple_of(lax.rem(colour_ref[0] + step, 4) * (D // 4), D // 4)

    query = jnp.zeros((128, HD), f32)
    squares = jnp.zeros((128, 1), f32)
    for step, ref in enumerate((mine_ref, one_ref, two_ref, three_ref)):
        part, more = gained(ref, gain_ref, start_of(step))
        squares = squares + more
        rows = query_weight_ref[pl.ds(start_of(step), D // 4), :]
        query = query + jnp.dot(part, rows, preferred_element_type=f32)
    scale = lax.rsqrt(squares / D + eps)
    query = (query * scale).astype(bf16)
    both = jnp.dot(pick_ref[...], served_ref[...], preferred_element_type=f32)
    scale = jnp.broadcast_to(scale, (128, 128)).T
    key_t = (both[:128] * scale).astype(bf16)
    value_t = (both[128:] * scale).astype(bf16)
    scores = jnp.dot(query, key_t, preferred_element_type=f32) * (1.0 / np.sqrt(np.float32(HD)))
    rows = lax.broadcasted_iota(jnp.int32, (128, 128), 0)
    columns = lax.broadcasted_iota(jnp.int32, (128, 128), 1)
    seg = jnp.broadcast_to(seg_ref[...].astype(f32), (128, 128))
    allowed = (rows >= columns) & (seg == seg.T)
    scores = jnp.where(allowed, scores, -1e30)
    weights = jnp.exp(scores - jnp.max(scores, axis=1, keepdims=True))
    weights = (weights / jnp.sum(weights, axis=1, keepdims=True)).astype(bf16)
    context = lax.dot_general(weights, value_t, (((1,), (1,)), ((), ())), preferred_element_type=f32).astype(bf16)
    refs = (own_ref, send_one_ref, send_two_ref, send_three_ref)
    for step in range(4):
        for z in range(8):
            at = pl.multiple_of(start_of(step) + z * 256, 256)
            product = jnp.dot(context, output_weight_ref[:, pl.ds(at, 256)], preferred_element_type=f32)
            for yl in range(2):
                ref = refs[(step + 2 * yl) % 4]
                ref[yl * 8 + z] = product[:, yl * 128 : yl * 128 + 128].astype(ref.dtype)


def project(
    colour_ref, columns_ref, raw_ref, gain_ref, projector_ref, own_ref, send_one_ref, send_two_ref, send_three_ref
):
    summed = jnp.zeros((128, HD), f32)
    for device in range(16):
        summed = summed + columns_ref[device].astype(f32)
    resid = raw_ref[...].astype(f32) + summed
    squares = jnp.sum(resid * resid, axis=1, keepdims=True)
    high = squares.astype(bf16)
    low = (squares - high.astype(f32)).astype(bf16)
    lane = lax.broadcasted_iota(jnp.int32, (128, 128), 1)
    tail = jnp.where(lane == 0, high.astype(f32), jnp.where(lane == 1, low.astype(f32), 0.0)).astype(bf16)
    features = (resid * gain_ref[...]).astype(bf16)
    row = lax.broadcasted_iota(jnp.int32, (128, 128), 0)
    yl = (row >> 4) & 1
    x = (colour_ref[0] + (row >> 5) + 2 * yl) & 3
    token = 32 * x + 4 * ((row >> 1) & 7) + 2 * yl + (row & 1)
    order = jnp.where(lane == token, 1.0, 0.0).astype(bf16)
    features = jnp.dot(order, features, preferred_element_type=f32).astype(bf16)
    tail = jnp.dot(order, tail, preferred_element_type=f32)
    for start in range(0, WIDTH + 128, 512):
        at = pl.ds(start, min(512, WIDTH + 128 - start))
        product = tail if start == WIDTH else jnp.dot(features, projector_ref[:, at], preferred_element_type=f32)
        own_ref[:, at] = product[:32]
        send_one_ref[:, at] = product[32:64].astype(bf16)
        send_two_ref[:, at] = product[64:96].astype(bf16)
        send_three_ref[:, at] = product[96:].astype(bf16)


def same_colour():
    def index(x, z, yl):
        return x * 16 + z * 2 + yl

    return [
        [index(c, z, 0) for z in range(8)] + [index((c + 2) % 4, z, 1) for z in range(8)] for c in range(4)
    ]


def same_quarter():
    return [[c * 8 + quarter + 4 * half for c in range(32) for half in range(2)] for quarter in range(4)]


def add_rows(own_ref, one_ref, two_ref, three_ref, out_ref):
    total = own_ref[...] + one_ref[...].astype(f32) + two_ref[...].astype(f32) + three_ref[...].astype(f32)
    squares = jnp.sum(total[:, WIDTH:], axis=1, keepdims=True)
    high = squares.astype(bf16).astype(f32)
    lane = lax.broadcasted_iota(jnp.int32, (32, 128), 1)
    tail = jnp.where(lane == 0, high, jnp.where(lane == 1, squares - high, 0.0))
    total = jnp.concatenate([total[:, :WIDTH], tail], axis=1)
    for device in range(16):
        out_ref[device] = total[2 * device : 2 * device + 2].astype(bf16)


def spread(tokens_ref, out_ref):
    for colour in range(4):
        block = tokens_ref[:, colour * (D // 4) : (colour + 1) * (D // 4)]
        for z in range(8):
            for yl in range(2):
                out_ref[(colour + 2 * yl) % 4 * 16 + z * 2 + yl] = block


def vmem_call(kernel, ins, outs, flops):
    vmem = pl.BlockSpec(memory_space=pltpu.VMEM)
    return pl.pallas_call(
        kernel,
        out_shape=[jax.ShapeDtypeStruct(*out) for out in outs],
        in_specs=[pl.BlockSpec(memory_space=pltpu.SMEM)] + [vmem] * ins,
        out_specs=[vmem] * len(outs),
        compiler_params=pltpu.CompilerParams(vmem_limit_bytes=VMEM_MB * 2**20),
        cost_estimate=pl.CostEstimate(flops=flops, bytes_accessed=2**22, transcendentals=0),
        name=kernel.__name__,
    )


def shards(
    tokens,
    sequence_numbers,
    query_projection_weight,
    key_projection_weight,
    value_projection_weight,
    output_projection_weight,
    attention_norm_gain,
    closing_norm_gain,
    projector,
    student_hidden_rows,
    student_norm_gain,
    adapter_down_map,
    adapter_up_map,
):
    tp_index = lax.axis_index(TP)
    colour = lax.rem(lax.axis_index("x") + 2 * lax.axis_index("yl"), 4)

    with jax.named_scope("tokens"):
        (by_colour,) = pl.pallas_call(
            spread,
            out_shape=[jax.ShapeDtypeStruct((64, 2, D // 4), bf16)],
            in_specs=[pl.BlockSpec(memory_space=pltpu.VMEM)],
            out_specs=[pl.BlockSpec(memory_space=pltpu.VMEM)],
            compiler_params=pltpu.CompilerParams(vmem_limit_bytes=VMEM_MB * 2**20),
        )(tokens)
        by_colour, key_columns, value_columns = lax.optimization_barrier(
            (by_colour, key_projection_weight, value_projection_weight)
        )
        mine = exchange(by_colour, TP).reshape(128, D // 4)
        parts = [mine, from_x(mine, 1), from_yl(mine), from_x(mine, 3)]
        at = lax.rem(tp_index, 16) * HD
        raw_cols = jnp.where(
            lax.axis_index("yl") == 0,
            lax.dynamic_slice_in_dim(parts[0], at, HD, 1),
            lax.dynamic_slice_in_dim(parts[2], at, HD, 1),
        )

    with jax.named_scope("kv_weights"):
        columns = jnp.stack([key_columns.T, value_columns.T]).reshape(2, 2, KV, D)

        def features(step):
            return lax.dynamic_slice_in_dim(columns, lax.rem(colour + step, 4) * (D // 4), D // 4, 3)

        kv = [features(step).reshape(32, D // 4) for step in range(4)]
        kv = [kv[0], from_x(kv[1], 3), from_yl(kv[2]), from_x(kv[3], 1)]
        kv = jnp.stack(kv).reshape(16, KV, D // 4).transpose(1, 0, 2).reshape(128, D // 4)

    with jax.named_scope("own_quarter"):
        gain = attention_norm_gain.reshape(1, D)
        where = colour.reshape(1)
        (served,) = vmem_call(own_quarter, 3, [((64, 16, 128), bf16)], flops=2**31)(where, mine, gain, kv)
        served = exchange(served, TP).reshape(1024, 128)

    with jax.named_scope("attention"):
        block = (16, 128, HD)
        total, *sent = vmem_call(attention, 10, [(block, f32)] + [(block, bf16)] * 3, flops=2**31)(
            where,
            *parts,
            gain,
            served,
            jnp.asarray(pick_rows(), bf16),
            sequence_numbers,
            query_projection_weight,
            output_projection_weight,
        )

    with jax.named_scope("output"):
        total = total + from_x(sent[0], 3).astype(f32) + from_yl(sent[1]).astype(f32) + from_x(sent[2], 1).astype(f32)
        columns = lax.all_to_all(
            total.astype(bf16), TP, split_axis=0, concat_axis=0, axis_index_groups=same_colour(), tiled=True
        )

    with jax.named_scope("target"):
        gain_cols = lax.dynamic_slice_in_dim(closing_norm_gain, tp_index * HD, HD, 0).reshape(1, HD)
        total, *sent = vmem_call(
            project, 4, [((32, WIDTH + 128), f32)] + [((32, WIDTH + 128), bf16)] * 3, flops=2**31
        )(where, columns, raw_cols, gain_cols, projector)
        received = from_x(sent[0], 3), from_yl(sent[1]), from_x(sent[2], 1)
        (rows_out,) = pl.pallas_call(
            add_rows,
            out_shape=[jax.ShapeDtypeStruct((16, 2, WIDTH + 128), bf16)],
            in_specs=[pl.BlockSpec(memory_space=pltpu.VMEM)] * 4,
            out_specs=[pl.BlockSpec(memory_space=pltpu.VMEM)],
            compiler_params=pltpu.CompilerParams(vmem_limit_bytes=VMEM_MB * 2**20),
        )(total, *received)
        rows_in = lax.all_to_all(rows_out, TP, split_axis=0, concat_axis=0, axis_index_groups=same_colour(), tiled=True)
        rows_in = jnp.sum(rows_in.astype(f32), axis=0)
        squares = rows_in[:, WIDTH] + rows_in[:, WIDTH + 1]
        target = rows_in[:, :WIDTH] * lax.rsqrt(squares / D + eps)[:, None]

    with jax.named_scope("student"):
        student = student_hidden_rows.astype(f32)
        student_normed = rms_norm(student, student_norm_gain).astype(bf16)
        lowrank = jnp.dot(student_normed, adapter_down_map, preferred_element_type=f32).astype(bf16)
        reached = student + jnp.dot(lowrank, adapter_up_map, preferred_element_type=f32)
        diff = reached - target
        token_loss = jnp.mean(diff * diff, axis=1)
        scaled = diff / jnp.sqrt(f32(512))
        back = lax.dot_general(
            scaled, adapter_up_map.astype(f32), (((1,), (1,)), ((), ())), precision=highest, preferred_element_type=f32
        )

    with jax.named_scope("columns"):

        def groups(v):
            return v.reshape(2, 28, 128).transpose(1, 0, 2)

        right = jnp.concatenate([back.astype(bf16), lowrank], axis=1)
        message = jnp.concatenate(
            [
                jnp.pad(jnp.concatenate([groups(student_normed), groups(scaled.astype(bf16))], axis=2), ((0, 4), (0, 0), (0, 0))),
                jnp.broadcast_to(right, (32, 2, 128)),
            ],
            axis=2,
        )
        message = jnp.broadcast_to(message[:, None], (32, 2, 2, 384)).reshape(64, 2, 384)
        message = lax.all_to_all(
            message, WIDE + ("z",), split_axis=0, concat_axis=0, axis_index_groups=same_quarter(), tiled=True
        ).reshape(128, 384)

        def product(left, right):
            return lax.dot_general(left, right, (((0,), (0,)), ((), ())), preferred_element_type=f32)

        down = product(message[:, 256:320], message[:, :128])
        up = product(message[:, 320:], message[:, 128:256])
        part = jnp.concatenate([down, up], axis=0).astype(bf16)
        one, two, three = (from_z(part, step).astype(f32) for step in (1, 2, 7))
        chunk = ((part.astype(f32) + two) + (one + three)).astype(bf16)

    with jax.named_scope("gradients"):
        whole = exchange(jnp.broadcast_to(chunk, (32, 128, 128)), WIDE)[:28].astype(f32)
        grad_down = whole[:, :64].transpose(0, 2, 1).reshape(WIDTH, RANK)
        grad_up = whole[:, 64:].transpose(1, 0, 2).reshape(RANK, WIDTH)
    return (token_loss, grad_down, grad_up)


def solution(mesh):
    fine = Mesh(np.asarray(mesh.devices).reshape(2, 2, 4, 8, 2), ALL)
    return jax.shard_map(
        shards,
        mesh=fine,
        in_specs=(
            P(ALL, None),
            P(("yh", "core"), None),
            P(None, TP),
            P(None, TP),
            P(None, TP),
            P(TP, None),
            P(),
            P(),
            P(TP, None),
            P(ALL, None),
            P(),
            P(),
            P(),
        ),
        out_specs=(P(ALL), P(), P()),
        check_vma=False,
    )
```

```python
import jax
import jax.numpy as jnp
import numpy as np
from jax import lax
from jax.experimental import pallas as pl
from jax.experimental.pallas import tpu as pltpu
from jax.sharding import Mesh
from jax.sharding import PartitionSpec as P

D = 8192
H = 64
KV = 8
HD = 128
WIDTH = 3584
RANK = 64
TP = ("x", "z", "yl")
ALL = ("yh", "core", "x", "z", "yl")
WIDE = ("yh", "core", "x", "yl")

eps = 1e-06
VMEM_MB = 24
f32 = jnp.float32
bf16 = jnp.bfloat16
highest = lax.Precision.HIGHEST


def rms_norm(values, gain):
    mean_sq = jnp.mean(values * values, axis=-1, keepdims=True)
    return values * lax.rsqrt(mean_sq + eps) * gain


def exchange(blocks, axes):
    return lax.all_to_all(blocks, axes, split_axis=0, concat_axis=0, tiled=True)


def from_x(block, step):
    return lax.ppermute(block, "x", [((i + step) % 4, i) for i in range(4)])


def from_z(block, step):
    return lax.ppermute(block, "z", [((i + step) % 8, i) for i in range(8)])


def from_yl(block):
    return lax.ppermute(block, "yl", [(0, 1), (1, 0)])


def pick_rows():
    pick = np.zeros((2, 4, 8, 2, 2, 4, 8, 2, 4, 2, 2), np.float32)
    for x in range(4):
        for yl in range(2):
            for step, (sx, syl) in enumerate([(x, yl), ((x + 1) % 4, yl), (x, 1 - yl), ((x + 3) % 4, yl)]):
                for z in range(8):
                    for part in range(2):
                        for e in range(2):
                            pick[part, x, z, yl, e, sx, z, syl, step, part, e] = 1
    return pick.reshape(256, 1024)


def gained(part_ref, gain_ref, start):
    wide = part_ref[...].astype(f32)
    squares = jnp.sum(wide * wide, axis=1, keepdims=True)
    return (wide * gain_ref[:, pl.ds(start, D // 4)]).astype(bf16), squares


def own_quarter(colour_ref, mine_ref, gain_ref, kv_ref, served_ref):
    part, _ = gained(mine_ref, gain_ref, pl.multiple_of(colour_ref[0] * (D // 4), D // 4))
    served = lax.dot_general(kv_ref[...], part, (((1,), (1,)), ((), ())), preferred_element_type=f32).astype(bf16)
    for device in range(64):
        head = device // 8
        served_ref[device] = served[head * 16 : head * 16 + 16]


def attention(
    colour_ref,
    mine_ref,
    one_ref,
    two_ref,
    three_ref,
    gain_ref,
    served_ref,
    pick_ref,
    seg_ref,
    query_weight_ref,
    output_weight_ref,
    own_ref,
    send_one_ref,
    send_two_ref,
    send_three_ref,
):
    def start_of(step):
        return pl.multiple_of(lax.rem(colour_ref[0] + step, 4) * (D // 4), D // 4)

    query = jnp.zeros((128, HD), f32)
    squares = jnp.zeros((128, 1), f32)
    for step, ref in enumerate((mine_ref, one_ref, two_ref, three_ref)):
        part, more = gained(ref, gain_ref, start_of(step))
        squares = squares + more
        rows = query_weight_ref[pl.ds(start_of(step), D // 4), :]
        query = query + jnp.dot(part, rows, preferred_element_type=f32)
    scale = lax.rsqrt(squares / D + eps)
    query = (query * scale).astype(bf16)
    both = jnp.dot(pick_ref[...], served_ref[...], preferred_element_type=f32)
    scale = jnp.broadcast_to(scale, (128, 128)).T
    key_t = (both[:128] * scale).astype(bf16)
    value_t = (both[128:] * scale).astype(bf16)
    scores = jnp.dot(query, key_t, preferred_element_type=f32) * (1.0 / np.sqrt(np.float32(HD)))
    rows = lax.broadcasted_iota(jnp.int32, (128, 128), 0)
    columns = lax.broadcasted_iota(jnp.int32, (128, 128), 1)
    seg = jnp.broadcast_to(seg_ref[...].astype(f32), (128, 128))
    allowed = (rows >= columns) & (seg == seg.T)
    scores = jnp.where(allowed, scores, -1e30)
    weights = jnp.exp(scores - jnp.max(scores, axis=1, keepdims=True))
    weights = (weights / jnp.sum(weights, axis=1, keepdims=True)).astype(bf16)
    context = lax.dot_general(weights, value_t, (((1,), (1,)), ((), ())), preferred_element_type=f32).astype(bf16)
    refs = (own_ref, send_one_ref, send_two_ref, send_three_ref)
    for step in range(4):
        for z in range(8):
            at = pl.multiple_of(start_of(step) + z * 256, 256)
            product = jnp.dot(context, output_weight_ref[:, pl.ds(at, 256)], preferred_element_type=f32)
            for yl in range(2):
                ref = refs[(step + 2 * yl + z) % 4]
                ref[yl * 8 + z] = product[:, yl * 128 : yl * 128 + 128].astype(ref.dtype)


def project(
    colour_ref, columns_ref, raw_ref, gain_ref, projector_ref, own_ref, send_one_ref, send_two_ref, send_three_ref
):
    summed = jnp.zeros((128, HD), f32)
    for device in range(16):
        summed = summed + columns_ref[device].astype(f32)
    resid = raw_ref[...].astype(f32) + summed
    squares = jnp.sum(resid * resid, axis=1, keepdims=True)
    high = squares.astype(bf16)
    low = (squares - high.astype(f32)).astype(bf16)
    lane = lax.broadcasted_iota(jnp.int32, (128, 128), 1)
    tail = jnp.where(lane == 0, high.astype(f32), jnp.where(lane == 1, low.astype(f32), 0.0)).astype(bf16)
    features = (resid * gain_ref[...]).astype(bf16)
    row = lax.broadcasted_iota(jnp.int32, (128, 128), 0)
    yl = (row >> 4) & 1
    z = (row >> 1) & 7
    x = (colour_ref[0] + (row >> 5) + 2 * yl + 8 - z) & 3
    token = 32 * x + 4 * z + 2 * yl + (row & 1)
    order = jnp.where(lane == token, 1.0, 0.0).astype(bf16)
    features = jnp.dot(order, features, preferred_element_type=f32).astype(bf16)
    tail = jnp.dot(order, tail, preferred_element_type=f32)
    for start in range(0, WIDTH + 128, 512):
        at = pl.ds(start, min(512, WIDTH + 128 - start))
        product = tail if start == WIDTH else jnp.dot(features, projector_ref[:, at], preferred_element_type=f32)
        own_ref[:, at] = product[:32]
        send_one_ref[:, at] = product[32:64].astype(bf16)
        send_two_ref[:, at] = product[64:96].astype(bf16)
        send_three_ref[:, at] = product[96:].astype(bf16)


def same_colour():
    def index(x, z, yl):
        return x * 16 + z * 2 + yl

    return [[index((c + 2 * yl - z) % 4, z, yl) for yl in range(2) for z in range(8)] for c in range(4)]


def same_quarter():
    return [[c * 8 + quarter + 4 * half for c in range(32) for half in range(2)] for quarter in range(4)]


def add_rows(own_ref, one_ref, two_ref, three_ref, out_ref):
    total = own_ref[...] + one_ref[...].astype(f32) + two_ref[...].astype(f32) + three_ref[...].astype(f32)
    squares = jnp.sum(total[:, WIDTH:], axis=1, keepdims=True)
    high = squares.astype(bf16).astype(f32)
    lane = lax.broadcasted_iota(jnp.int32, (32, 128), 1)
    tail = jnp.where(lane == 0, high, jnp.where(lane == 1, squares - high, 0.0))
    total = jnp.concatenate([total[:, :WIDTH], tail], axis=1)
    for device in range(16):
        out_ref[device] = total[2 * device : 2 * device + 2].astype(bf16)


def spread(tokens_ref, out_ref):
    for colour in range(4):
        block = tokens_ref[:, colour * (D // 4) : (colour + 1) * (D // 4)]
        for z in range(8):
            for yl in range(2):
                out_ref[(colour + 2 * yl - z) % 4 * 16 + z * 2 + yl] = block


def vmem_call(kernel, ins, outs, flops):
    vmem = pl.BlockSpec(memory_space=pltpu.VMEM)
    return pl.pallas_call(
        kernel,
        out_shape=[jax.ShapeDtypeStruct(*out) for out in outs],
        in_specs=[pl.BlockSpec(memory_space=pltpu.SMEM)] + [vmem] * ins,
        out_specs=[vmem] * len(outs),
        compiler_params=pltpu.CompilerParams(vmem_limit_bytes=VMEM_MB * 2**20),
        cost_estimate=pl.CostEstimate(flops=flops, bytes_accessed=2**22, transcendentals=0),
        name=kernel.__name__,
    )


def shards(
    tokens,
    sequence_numbers,
    query_projection_weight,
    key_projection_weight,
    value_projection_weight,
    output_projection_weight,
    attention_norm_gain,
    closing_norm_gain,
    projector,
    student_hidden_rows,
    student_norm_gain,
    adapter_down_map,
    adapter_up_map,
):
    tp_index = lax.axis_index(TP)
    colour = lax.rem(lax.axis_index("x") + 2 * lax.axis_index("yl") + lax.axis_index("z"), 4)

    with jax.named_scope("tokens"):
        (by_colour,) = pl.pallas_call(
            spread,
            out_shape=[jax.ShapeDtypeStruct((64, 2, D // 4), bf16)],
            in_specs=[pl.BlockSpec(memory_space=pltpu.VMEM)],
            out_specs=[pl.BlockSpec(memory_space=pltpu.VMEM)],
            compiler_params=pltpu.CompilerParams(vmem_limit_bytes=VMEM_MB * 2**20),
        )(tokens)
        by_colour, key_columns, value_columns = lax.optimization_barrier(
            (by_colour, key_projection_weight, value_projection_weight)
        )
        mine = exchange(by_colour, TP).reshape(128, D // 4)
        parts = [mine, from_x(mine, 1), from_yl(mine), from_x(mine, 3)]
        at = lax.rem(tp_index, 16) * HD
        step = lax.rem(lax.axis_index("x") + 4 - colour, 4)
        raw_cols = lax.select_n(step, *[lax.dynamic_slice_in_dim(part, at, HD, 1) for part in parts])

    with jax.named_scope("kv_weights"):
        columns = jnp.stack([key_columns.T, value_columns.T]).reshape(2, 2, KV, D)

        def features(step):
            return lax.dynamic_slice_in_dim(columns, lax.rem(colour + step, 4) * (D // 4), D // 4, 3)

        kv = [features(step).reshape(32, D // 4) for step in range(4)]
        kv = [kv[0], from_x(kv[1], 3), from_yl(kv[2]), from_x(kv[3], 1)]
        kv = jnp.stack(kv).reshape(16, KV, D // 4).transpose(1, 0, 2).reshape(128, D // 4)

    with jax.named_scope("own_quarter"):
        gain = attention_norm_gain.reshape(1, D)
        where = colour.reshape(1)
        (served,) = vmem_call(own_quarter, 3, [((64, 16, 128), bf16)], flops=2**31)(where, mine, gain, kv)
        served = exchange(served, TP).reshape(1024, 128)

    with jax.named_scope("attention"):
        block = (16, 128, HD)
        total, *sent = vmem_call(attention, 10, [(block, f32)] + [(block, bf16)] * 3, flops=2**31)(
            where,
            *parts,
            gain,
            served,
            jnp.asarray(pick_rows(), bf16),
            sequence_numbers,
            query_projection_weight,
            output_projection_weight,
        )

    with jax.named_scope("output"):
        total = total + from_x(sent[0], 3).astype(f32) + from_yl(sent[1]).astype(f32) + from_x(sent[2], 1).astype(f32)
        columns = lax.all_to_all(
            total.astype(bf16), TP, split_axis=0, concat_axis=0, axis_index_groups=same_colour(), tiled=True
        )

    with jax.named_scope("target"):
        gain_cols = lax.dynamic_slice_in_dim(closing_norm_gain, tp_index * HD, HD, 0).reshape(1, HD)
        total, *sent = vmem_call(
            project, 4, [((32, WIDTH + 128), f32)] + [((32, WIDTH + 128), bf16)] * 3, flops=2**31
        )(where, columns, raw_cols, gain_cols, projector)
        received = from_x(sent[0], 3), from_yl(sent[1]), from_x(sent[2], 1)
        (rows_out,) = pl.pallas_call(
            add_rows,
            out_shape=[jax.ShapeDtypeStruct((16, 2, WIDTH + 128), bf16)],
            in_specs=[pl.BlockSpec(memory_space=pltpu.VMEM)] * 4,
            out_specs=[pl.BlockSpec(memory_space=pltpu.VMEM)],
            compiler_params=pltpu.CompilerParams(vmem_limit_bytes=VMEM_MB * 2**20),
        )(total, *received)
        rows_in = lax.all_to_all(rows_out, TP, split_axis=0, concat_axis=0, axis_index_groups=same_colour(), tiled=True)
        rows_in = jnp.sum(rows_in.astype(f32), axis=0)
        squares = rows_in[:, WIDTH] + rows_in[:, WIDTH + 1]
        target = rows_in[:, :WIDTH] * lax.rsqrt(squares / D + eps)[:, None]

    with jax.named_scope("student"):
        student = student_hidden_rows.astype(f32)
        student_normed = rms_norm(student, student_norm_gain).astype(bf16)
        lowrank = jnp.dot(student_normed, adapter_down_map, preferred_element_type=f32).astype(bf16)
        reached = student + jnp.dot(lowrank, adapter_up_map, preferred_element_type=f32)
        diff = reached - target
        token_loss = jnp.mean(diff * diff, axis=1)
        scaled = diff / jnp.sqrt(f32(512))
        back = lax.dot_general(
            scaled, adapter_up_map.astype(f32), (((1,), (1,)), ((), ())), precision=highest, preferred_element_type=f32
        )

    with jax.named_scope("columns"):

        def groups(v):
            return v.reshape(2, 28, 128).transpose(1, 0, 2)

        right = jnp.concatenate([back.astype(bf16), lowrank], axis=1)
        message = jnp.concatenate(
            [
                jnp.pad(jnp.concatenate([groups(student_normed), groups(scaled.astype(bf16))], axis=2), ((0, 4), (0, 0), (0, 0))),
                jnp.broadcast_to(right, (32, 2, 128)),
            ],
            axis=2,
        )
        message = jnp.broadcast_to(message[:, None], (32, 2, 2, 384)).reshape(64, 2, 384)
        message = lax.all_to_all(
            message, WIDE + ("z",), split_axis=0, concat_axis=0, axis_index_groups=same_quarter(), tiled=True
        ).reshape(128, 384)

        def product(left, right):
            return lax.dot_general(left, right, (((0,), (0,)), ((), ())), preferred_element_type=f32)

        down = product(message[:, 256:320], message[:, :128])
        up = product(message[:, 320:], message[:, 128:256])
        part = jnp.concatenate([down, up], axis=0).astype(bf16)
        one, two, three = (from_z(part, step).astype(f32) for step in (1, 2, 7))
        chunk = ((part.astype(f32) + two) + (one + three)).astype(bf16)

    with jax.named_scope("gradients"):
        whole = exchange(jnp.broadcast_to(chunk, (32, 128, 128)), WIDE)[:28].astype(f32)
        grad_down = whole[:, :64].transpose(0, 2, 1).reshape(WIDTH, RANK)
        grad_up = whole[:, 64:].transpose(1, 0, 2).reshape(RANK, WIDTH)
    return (token_loss, grad_down, grad_up)


def solution(mesh):
    fine = Mesh(np.asarray(mesh.devices).reshape(2, 2, 4, 8, 2), ALL)
    return jax.shard_map(
        shards,
        mesh=fine,
        in_specs=(
            P(ALL, None),
            P(("yh", "core"), None),
            P(None, TP),
            P(None, TP),
            P(None, TP),
            P(TP, None),
            P(),
            P(),
            P(TP, None),
            P(ALL, None),
            P(),
            P(),
            P(),
        ),
        out_specs=(P(ALL), P(), P()),
        check_vma=False,
    )
```
